256 devices in a mesh: leaf: 64 (over y_lo, x, z), blk: 4 (over y_hi, core).
Axes of the slice: x: 4, y: 4 (y_hi: 2, y_lo: 2; y = y_hi * 2 + y_lo), z: 8, core: 2. Of those that a mesh axis runs over, the one named last changes fastest.
Arguments:
- root_front_inverse: float32 [2048, 2048], P('leaf', 'blk'), as said below
- child_front_inverse: float32 [65536, 1024], P('leaf', 'blk'), as said below
- child_coupling_block: float32 [32768, 1024], P('leaf', 'blk'), may hold values from -0.375 to 0.375
- coupled_root_blocks: int32 [64, 4], P('leaf'), may hold values from 0 to 15, as said below
- jacobian_child_index: int32 [6, 131072], P(None, ('leaf', 'blk')), may hold values from 0 to 1023
- jacobian_child_value: float32 [6, 131072], P(None, ('leaf', 'blk')), may hold values from -6 to 6
- jacobian_root_index: int32 [2, 131072], P(None, ('leaf', 'blk')), may hold values from 0 to 511
- jacobian_root_value: float32 [2, 131072], P(None, ('leaf', 'blk')), may hold values from -6 to 6
- resid: float32 [131072], P(('leaf', 'blk')), may hold values from -6 to 6
- noise_variance: float32 [131072], P(('leaf', 'blk')), may hold values from 0.05 to 1
- device_active_count: int32 [256], P(('leaf', 'blk')), may hold values from 1 to 512, 65536 in all
Outputs:
- normalized: float32 [131072], P(('leaf', 'blk'))
The draws below stay inside these ranges and needn't reach their ends.
Inputs may be any that keep to these rules, and one draw needn't show every extreme that they name: root_front_inverse is lower triangular with a positive diagonal. Each 1024 x 1024 block of child_front_inverse is lower triangular with a positive diagonal. `coupled_root_blocks`: each row names 4 different root blocks.
All inputs are finite; a program needn't handle non-finite values. No bound on the sum of `device_active_count` on one device may be relied on, other than what follows from the above.
Results may differ from the reference program's by a relative error of at most 0.0003.
Values sent between devices are 32-bit elements; how exact they have to be, the bound alone decides.
A program may use at most 64 MiB of HBM per device.

```python
import math
import jax
import jax.numpy as jnp
import numpy as np
from jax import lax

W = 2048
B = 128
KB = 4
CHILD_WIDTH = 1024
DEVICE_SLOTS = 512
CHILD_ENTRIES = 6
ROOT_ENTRIES = 2
NB = 16
COUPLED_ROOTROWS = 512
CROWS = 65536
OROWS = 32768
MEASUREMENT_ALL = 131072
N_LEAF = 64
N_BLK = 4
DEVICES = 256


def triangle(key, rows, cols):
    key_diag = jax.random.fold_in(key, 11)
    key_off = jax.random.fold_in(key, 12)
    diag = jax.random.uniform(key_diag, (rows, cols), jnp.float32, 1.0, 2.0)
    off = jax.random.normal(key_off, (rows, cols), jnp.float32) * (2.0 / cols ** 0.5)
    row_pos = jnp.arange(rows, dtype=jnp.int32)[:, None] % cols
    col_pos = jnp.arange(cols, dtype=jnp.int32)[None, :]
    return jnp.where(row_pos > col_pos, off, jnp.where(row_pos == col_pos, diag, jnp.float32(0.0)))


def draw_root_front_inverse(key, part):
    return triangle(key, W, W)


def draw_child_front_inverse(key, part):
    return triangle(key, CROWS, CHILD_WIDTH)


def draw_coupled_root_blocks(key, part):
    keys = jax.random.split(jax.random.fold_in(key, 21), N_LEAF)

    def pick(one_key):
        return jax.random.permutation(one_key, NB)[:KB].astype(jnp.int32)
    return jax.vmap(pick)(keys)


def plant(values, key, smallest, largest):
    extent = values.shape
    spot = [jax.random.randint(jax.random.fold_in(key, axis), (), 0, extent[axis]) for axis in range(len(extent))]
    values = values.at[tuple(spot)].set(smallest)
    longest = extent.index(max(extent))
    spot[longest] = (spot[longest] + 1) % extent[longest]
    return values.at[tuple(spot)].set(largest)


def level_of(stream_key, extent, cuts, least, top_value):
    gain, own = 1.0, jax.random.fold_in(stream_key, 6)
    for dim, shards_of in cuts:
        steps = jnp.exp(jax.random.uniform(jax.random.fold_in(own, dim), (shards_of,), jnp.float32, least / len(cuts), top_value / len(cuts)))
        gain = gain * jnp.repeat(steps, extent[dim] // shards_of).reshape([-1 if axis == dim else 1 for axis in range(len(extent))])
    return gain


def length_profile(number_of, total, limit, lean):
    portions = [(1 << 20) // math.isqrt(rank ** lean) + 1 for rank in range(2, number_of + 1)]
    spare, given = total - limit - (number_of - 1), [1] * (number_of - 1)
    while spare > 0:
        free = [i for i in range(number_of - 1) if given[i] < limit]
        pool, remaining = sum([portions[i] for i in free]), spare
        for i in free:
            more = min(limit - given[i], max(1, remaining * portions[i] // pool), spare)
            given[i] = given[i] + more
            spare = spare - more
    return np.array([limit] + given)


def ragged(stream_key, amount, total, reach, slope):
    if amount == 2:
        one = jax.random.randint(stream_key, (), max(1, total - reach), min(reach, total - 1) + 1)
        return jnp.stack([one, total - one])
    sizes = jnp.asarray(length_profile(amount, total, reach, slope), jnp.int32)
    pairs = (amount - 1) // 2
    source_of, sink = sizes[1:1 + 2 * pairs:2], sizes[2:2 + 2 * pairs:2]
    room = jnp.minimum(source_of - 1, reach - sink)
    moved = jax.random.randint(jax.random.fold_in(stream_key, 1), (pairs,), 0, 1 << 20) % (room + 1)
    sizes = sizes.at[1:1 + 2 * pairs:2].set(source_of - moved).at[2:2 + 2 * pairs:2].set(sink + moved)
    return sizes[jax.random.permutation(jax.random.fold_in(stream_key, 2), amount)]


def scatter_about(stream_key, extent, deviation, limit, pieces=(), kind=jnp.bfloat16):
    entries = jax.random.normal(stream_key, extent, jnp.float32) * deviation
    if len(pieces) > 0:
        entries = level_of(stream_key, extent, pieces, -0.22, 0.18) * entries
    return jnp.clip(entries, min=-limit, max=limit).astype(kind)


def setup_inputs(seed: int = 0) -> dict:
    key_of = jax.random.split(jax.random.key(seed), 12)
    root_front_inverse = draw_root_front_inverse(jax.random.fold_in(key_of[11], 71), 0)
    child_front_inverse = draw_child_front_inverse(jax.random.fold_in(key_of[11], 71), 0)
    child_coupling_block = scatter_about(key_of[2], (OROWS, CHILD_WIDTH), (CHILD_WIDTH // 4) ** -0.5, 0.375, ((0, 64), (1, 4)), jnp.float32)
    coupled_root_blocks = draw_coupled_root_blocks(jax.random.fold_in(key_of[11], 71), 0)
    jacobian_child_index = plant(jax.random.randint(key_of[4], (CHILD_ENTRIES, MEASUREMENT_ALL), 0, CHILD_WIDTH), jax.random.fold_in(key_of[4], 1), 0, CHILD_WIDTH - 1).astype(jnp.int32)
    jacobian_child_value = scatter_about(key_of[5], (CHILD_ENTRIES, MEASUREMENT_ALL), 1.0, 6.0, ((1, 256),), jnp.float32)
    jacobian_root_index = plant(jax.random.randint(key_of[6], (ROOT_ENTRIES, MEASUREMENT_ALL), 0, COUPLED_ROOTROWS), jax.random.fold_in(key_of[6], 1), 0, COUPLED_ROOTROWS - 1).astype(jnp.int32)
    jacobian_root_value = scatter_about(key_of[7], (ROOT_ENTRIES, MEASUREMENT_ALL), 1.0, 6.0, ((1, 256),), jnp.float32)
    resid = scatter_about(key_of[8], (MEASUREMENT_ALL,), 1.0, 6.0, ((0, 256),), jnp.float32)
    noise_variance = jnp.clip(jnp.exp(math.log(1.0) - 2.9957323 * jax.random.uniform(key_of[9], (MEASUREMENT_ALL,), jnp.float32) ** level_of(key_of[9], (MEASUREMENT_ALL,), ((0, 256),), -0.2, 0.2)), 0.05, 1.0)
    device_active_count = ragged(key_of[10], DEVICES, DEVICES * DEVICE_SLOTS // 2, DEVICE_SLOTS, 2).astype(jnp.int32)
    return dict(root_front_inverse=root_front_inverse, child_front_inverse=child_front_inverse, child_coupling_block=child_coupling_block, coupled_root_blocks=coupled_root_blocks, jacobian_child_index=jacobian_child_index, jacobian_child_value=jacobian_child_value, jacobian_root_index=jacobian_root_index, jacobian_root_value=jacobian_root_value, resid=resid, noise_variance=noise_variance, device_active_count=device_active_count)


def reference(root_front_inverse, child_front_inverse, child_coupling_block, coupled_root_blocks, jacobian_child_index, jacobian_child_value, jacobian_root_index, jacobian_root_value, resid, noise_variance, device_active_count):
    high = lax.Precision.HIGHEST
    sigma_root = jnp.dot(root_front_inverse.T, root_front_inverse, precision=high, preferred_element_type=jnp.float32)
    offsets = jnp.arange(COUPLED_ROOTROWS, dtype=jnp.int32)
    per_child = N_BLK * DEVICE_SLOTS

    def one_child(child):
        rows_need = (coupled_root_blocks[child][offsets // B] * B + offsets % B).astype(jnp.int32)
        ancestor = jnp.take(jnp.take(sigma_root, rows_need, axis=0), rows_need, axis=1)
        inv_block = lax.dynamic_slice_in_dim(child_front_inverse, (child * CHILD_WIDTH).astype(jnp.int32), CHILD_WIDTH, 0)
        off_block = lax.dynamic_slice_in_dim(child_coupling_block, (child * COUPLED_ROOTROWS).astype(jnp.int32), COUPLED_ROOTROWS, 0)
        first = (child * per_child).astype(jnp.int32)
        jidx = lax.dynamic_slice_in_dim(jacobian_child_index, first, per_child, 1)
        jval = lax.dynamic_slice_in_dim(jacobian_child_value, first, per_child, 1)
        ridx = lax.dynamic_slice_in_dim(jacobian_root_index, first, per_child, 1)
        rval = lax.dynamic_slice_in_dim(jacobian_root_value, first, per_child, 1)
        noise = lax.dynamic_slice_in_dim(noise_variance, first, per_child, 0)
        inv_cols = jnp.zeros((CHILD_WIDTH, per_child), jnp.float32)
        for k in range(CHILD_ENTRIES):
            inv_cols = inv_cols + jnp.take(inv_block, jidx[k], axis=1) * jval[k][None, :]
        root_part = jnp.zeros((COUPLED_ROOTROWS, per_child), jnp.float32)
        for k in range(ROOT_ENTRIES):
            root_part = root_part + jnp.where(offsets[:, None] == ridx[k][None, :], rval[k][None, :], jnp.float32(0.0))
        gap = jnp.dot(off_block, inv_cols, precision=high, preferred_element_type=jnp.float32) - root_part
        weighted = jnp.dot(ancestor, gap, precision=high, preferred_element_type=jnp.float32)
        return noise + lax.optimization_barrier(jnp.sum(inv_cols * inv_cols, axis=0)) + lax.optimization_barrier(jnp.sum(gap * weighted, axis=0))
    omega = lax.map(one_child, jnp.arange(N_LEAF, dtype=jnp.int32)).reshape(-1)
    slot_positions = jnp.arange(MEASUREMENT_ALL, dtype=jnp.int32)
    active_slot_mask = slot_positions % DEVICE_SLOTS < jnp.take(device_active_count, slot_positions // DEVICE_SLOTS)
    return jnp.where(active_slot_mask, resid / jnp.sqrt(omega), jnp.float32(0.0))
```

```python
import functools

import jax
import jax.numpy as jnp
from jax import lax
from jax.experimental import pallas as pl
from jax.experimental.pallas import tpu as pltpu
from jax.sharding import PartitionSpec as P

MESH = pl.DeviceIdType.MESH
HIGH = lax.Precision.HIGHEST
TILES = 18


def dot(a, b):
    return jnp.dot(a, b, precision=HIGH, preferred_element_type=jnp.float32)


def dot_t(a, b):
    return lax.dot_general(
        a, b, (((0,), (0,)), ((), ())), precision=HIGH, preferred_element_type=jnp.float32
    )


def kernel(
    l_ref, f_ref, c_ref, sel_ref, jci_ref, jcv_ref, jri_ref, jrv_ref, resid_ref, noise_ref, count_ref,
    out_ref,
    l_buf, z_own, z_oth, f_buf, c_buf, j_buf, v_buf, g_buf, s_buf, a_send, a_recv, a_sum, sel_buf, sel_sm,
    l_send, l_recv, z_send, z_recv, d_send, d_recv, sel_send, sel_recv,
    fc_send, fc_recv, cc_send, cc_recv, x_send, x_recv, as_send, as_recv,
):
    leaf = lax.axis_index("leaf")
    blk = lax.axis_index("blk")
    ylo, x, z = lax.div(leaf, 32), lax.rem(lax.div(leaf, 8), 4), lax.rem(leaf, 8)
    yhi, core = lax.div(blk, 2), lax.rem(blk, 2)

    def device(ylo_d, x_d, z_d, blk_d):
        return {"leaf": ylo_d * 32 + x_d * 8 + z_d, "blk": blk_d}

    def copy(src, dst, send, recv, to):
        return pltpu.make_async_remote_copy(
            src_ref=src, dst_ref=dst, send_sem=send, recv_sem=recv, device_id=to, device_id_type=MESH
        )

    mirror = 3 - x
    zr, zl = lax.rem(z + 1, 8), lax.rem(z + 7, 8)
    right, left = device(ylo, x, zr, blk), device(ylo, x, zl, blk)
    mate_blk = 2 * yhi + 1 - core
    mate = device(ylo, x, z, mate_blk)
    across_blk = 2 * (1 - yhi) + core
    across = device(ylo, x, z, across_blk)
    far_blk = 2 * (1 - yhi) + 1 - core

    barrier = pltpu.get_barrier_semaphore()
    partners = [right, left]
    for ylo_d in range(2):
        for blk_d in range(4):
            partners.append(device(ylo_d, mirror, z, blk_d))
    for d_ylo in range(2):
        for d_blk in range(4):
            if (d_ylo, d_blk) != (0, 0):
                partners.append(device(lax.rem(ylo + d_ylo, 2), x, z, lax.rem(blk + d_blk, 4)))
    even = lax.rem(x, 2)
    other_near = lax.rem(x + jnp.where(even == 0, 1, 3), 4)
    partners.append(device(ylo, lax.rem(x + 2, 4), z, blk))
    partners.append(device(ylo, other_near, z, blk))
    for p in partners:
        pl.semaphore_signal(barrier, inc=1, device_id=p, device_id_type=MESH)
    pl.semaphore_wait(barrier, len(partners))

    for core_d in range(2):
        for h in range(2):
            for u in range(2):
                for q in range(2):
                    l_buf[core_d, h, u, q] = l_ref[
                        16 * core_d + 8 * u : 16 * core_d + 8 * u + 8, 256 * h + 128 * q : 256 * h + 128 * q + 128
                    ]
    upper = ylo == 0
    x_to = jnp.where(upper, x, mirror)
    for h in range(2):
        tile = 2 * blk + h
        slot = jnp.where(upper, tile, 4 - x + tile)
        valid = jnp.where(upper, tile <= x, tile <= 4 + x)
        for ylo_d in range(2):
            for blk_d in range(4):
                core_d = blk_d % 2
                src = l_buf.at[core_d, h]
                self_ = upper & (ylo_d == ylo) & (blk_d == blk)
                dst = z_own.at[0, :, pl.ds(2 * slot, 2)]

                @pl.when(valid & jnp.logical_not(self_))
                def _():
                    copy(
                        src, dst, l_send.at[h, ylo_d, blk_d], l_recv.at[slot],
                        device(ylo_d, x_to, z, blk_d),
                    ).start()

                @pl.when(valid & self_)
                def _():
                    pltpu.make_async_copy(src, dst, l_recv.at[slot]).start()

    sel_copies = []
    for d in range(1, 4):
        cp = copy(
            sel_ref, sel_buf.at[4 - d], sel_send.at[d], sel_recv.at[4 - d],
            device(ylo, lax.rem(x + d, 4), z, blk),
        )
        cp.start()
        sel_copies.append(cp)
    own_sel = pltpu.make_async_copy(sel_ref, sel_buf.at[0], sel_recv.at[0])
    own_sel.start()

    def f_rows(r):
        return pl.ds(256 * r, 256)

    def f_copy(kind, r):
        if kind == 0:
            return copy(f_ref.at[f_rows(r)], f_buf.at[blk, f_rows(r)], fc_send.at[0, r], fc_recv.at[0, r], mate)
        if kind == 1:
            return copy(f_ref.at[f_rows(r)], f_buf.at[blk, f_rows(r)], fc_send.at[1, r], fc_recv.at[1, r], across)
        return copy(
            f_buf.at[across_blk, f_rows(r)], f_buf.at[across_blk, f_rows(r)], fc_send.at[2, r], fc_recv.at[2, r], mate
        )

    def c_copy(kind, r):
        if kind == 0:
            return copy(c_ref.at[f_rows(r)], c_buf.at[blk, f_rows(r)], cc_send.at[0, r], cc_recv.at[0, r], mate)
        if kind == 1:
            return copy(c_ref.at[f_rows(r)], c_buf.at[blk, f_rows(r)], cc_send.at[1, r], cc_recv.at[1, r], across)
        return copy(
            c_buf.at[across_blk, f_rows(r)], c_buf.at[across_blk, f_rows(r)], cc_send.at[2, r], cc_recv.at[2, r], mate
        )

    f_own = [pltpu.make_async_copy(f_ref.at[f_rows(r)], f_buf.at[blk, f_rows(r)], fc_recv.at[3, r]) for r in range(4)]
    c_own = [pltpu.make_async_copy(c_ref.at[f_rows(r)], c_buf.at[blk, f_rows(r)], cc_recv.at[3, r]) for r in range(2)]

    for kind in (1, 0):
        for r in range(4):

            @pl.when(r >= blk)
            def _():
                f_copy(kind, r).start()

        for r in range(2):
            c_copy(kind, r).start()
    for r in range(4):

        @pl.when(r >= blk)
        def _():
            f_own[r].start()

    for r in range(2):
        c_own[r].start()

    @pl.loop(0, 16)
    def _(i):
        rows = lax.broadcasted_iota(jnp.int32, (64, 512), 0) + i * 64
        acc = jnp.zeros((64, 512), jnp.float32)
        for k in range(6):
            acc = acc + jnp.where(rows == jci_ref[k : k + 1, :], jcv_ref[k : k + 1, :], 0.0)
        j_buf[pl.ds(pl.multiple_of(i * 64, 64), 64), :] = acc

    for slot in range(9):
        tile = z_own.at[0, :, pl.ds(2 * slot, 2)]
        pltpu.make_async_copy(tile, tile, l_recv.at[slot]).wait()

    def sub(ref, s, u):
        return ref.at[s, u]

    z_copies = []

    def ring(s, u, way):
        to = s + 1 if way == 0 else (s + 7) % 8
        cp = copy(sub(z_own, s, u), sub(z_own, to, u), z_send.at[way, s, u], z_recv.at[to, u], right if way == 0 else left)
        cp.start()
        z_copies.append(cp)

    def share(s, u):
        cp = copy(sub(z_own, s, u), sub(z_oth, s, u), d_send.at[s, u], d_recv.at[s, u], mate)
        cp.start()
        return cp

    shares = []

    def arrived(s, u):
        pltpu.make_async_copy(sub(z_own, s, u), sub(z_own, s, u), z_recv.at[s, u]).wait()

    for u in range(2):
        ring(0, u, 0)
        ring(0, u, 1)
    for u in range(2):
        shares.append(share(0, u))
    for s in range(1, 4):
        for u in range(2):
            arrived(s, u)
            if s < 3 or u == 0:
                ring(s, u, 0)
            shares.append(share(s, u))
            arrived(8 - s, u)
            if s < 3 or u == 1:
                ring(8 - s, u, 1)
            shares.append(share(8 - s, u))
    for u in range(2):
        arrived(4, u)
        shares.append(share(4, u))
    for cp in sel_copies:
        cp.wait()
    own_sel.wait()
    pltpu.sync_copy(sel_buf, sel_sm)
    for cp in shares:
        cp.wait()

    x_copies = []
    for d in (2, 1, 3, 0):
        for i in range(4):
            j = sel_sm[d, lax.rem(i + core, 4), 0]
            choice = sel_buf[d, pl.ds(lax.rem(i + core, 4), 1), :]
            hi0 = 2 * x + 1
            hi1 = 15 - 2 * x
            below = 2 * (x + 1) + jnp.minimum(j, hi1)
            at = pl.ds(i * 128, 128)
            for n, ref in enumerate((z_own, z_oth)):
                part = ref[:, :, j].reshape(128, 128)
                s_buf[pl.ds(256 * n, 128), at] = jnp.where(choice <= hi0, part, 0.0)
                part = ref[:, :, below].reshape(128, 128)
                s_buf[pl.ds(256 * n + 128, 128), at] = jnp.where(choice <= hi1, part, 0.0)
        first = dot_t(s_buf[:, 0:128], s_buf[:, 0:384])
        second = dot_t(s_buf[:, 256:384], s_buf[:, 256:512])
        a_send[d, :, 0:128] = first[:, 0:128]
        a_send[d, :, 128:384] = 2.0 * first[:, 128:384]
        a_send[d, :, 384:512] = second[:, 0:128]
        a_send[d, :, 512:640] = 2.0 * second[:, 128:256]
        if d:
            cp = copy(
                a_send.at[d], a_recv.at[4 - d], x_send.at[d], x_recv.at[4 - d],
                device(ylo, lax.rem(x + d, 4), z, blk),
            )
            cp.start()
            x_copies.append(cp)

    for r in range(4):

        @pl.when(r >= across_blk)
        def _():
            f_copy(1, r).wait_recv()
            f_copy(2, r).start()

    for r in range(2):
        c_copy(1, r).wait_recv()
        c_copy(2, r).start()
    for r in range(4):

        @pl.when(r >= blk)
        def _():
            f_own[r].wait()

        @pl.when(r >= mate_blk)
        def _():
            f_copy(0, r).wait_recv()

        @pl.when(r >= far_blk)
        def _():
            f_copy(2, r).wait_recv()

    square = jnp.zeros((1, 512), jnp.float32)
    for r in range(4):
        acc = dot(f_buf[0, 256 * r : 256 * r + 256, :], j_buf[0:256, :])
        for s in range(1, r + 1):
            acc = acc + dot(f_buf[s, 256 * r : 256 * r + 256, :], j_buf[256 * s : 256 * s + 256, :])
        v_buf[256 * r : 256 * r + 256, :] = acc
        square = square + jnp.sum(acc * acc, axis=0, keepdims=True)

    for r in range(2):
        c_own[r].wait()
        c_copy(0, r).wait_recv()
        c_copy(2, r).wait_recv()
    for q in range(4):
        rows = lax.broadcasted_iota(jnp.int32, (128, 512), 0) + q * 128
        root = jnp.zeros((128, 512), jnp.float32)
        for k in range(2):
            root = root + jnp.where(rows == jri_ref[k : k + 1, :], jrv_ref[k : k + 1, :], 0.0)
        acc = dot(c_buf[0, 128 * q : 128 * q + 128, :], v_buf[0:256, :])
        for s in range(1, 4):
            acc = acc + dot(c_buf[s, 128 * q : 128 * q + 128, :], v_buf[256 * s : 256 * s + 256, :])
        acc = acc - root
        g_buf[128 * q : 128 * q + 128, :] = acc
        if q == 0:
            g_buf[512:640, :] = acc

    for cp in x_copies:
        cp.wait_recv()
    a_sum[0] = a_send[0] + a_recv[1] + a_recv[2] + a_recv[3]
    a_share = copy(a_sum.at[0], a_sum.at[1], as_send, as_recv, mate)
    a_share.start()

    def quad(n, c):
        start = pl.multiple_of(c * 128, 128)
        w = dot(a_sum[n, :, 0:384], g_buf[pl.ds(start, 384), :])
        q = jnp.sum(w * g_buf[pl.ds(start, 128), :], axis=0, keepdims=True)
        start = pl.multiple_of(c * 128 + 256, 128)
        w = dot(a_sum[n, :, 384:640], g_buf[pl.ds(start, 256), :])
        return q + jnp.sum(w * g_buf[pl.ds(start, 128), :], axis=0, keepdims=True)

    omega = noise_ref[...] + square + quad(0, core)
    a_share.wait()
    omega = omega + quad(1, 1 - core)
    live = lax.broadcasted_iota(jnp.int32, (1, 512), 1) < count_ref[0]
    out_ref[...] = jnp.where(live, resid_ref[...] / jnp.sqrt(omega), 0.0)

    for h in range(2):
        tile = 2 * blk + h
        valid = jnp.where(upper, tile <= x, tile <= 4 + x)
        for ylo_d in range(2):
            for blk_d in range(4):
                self_ = upper & (ylo_d == ylo) & (blk_d == blk)
                src = l_buf.at[0, h]

                @pl.when(valid & jnp.logical_not(self_))
                def _():
                    pltpu.make_async_copy(src, src, l_send.at[h, ylo_d, blk_d]).wait()

    for cp in z_copies:
        cp.wait_send()
    for cp in x_copies:
        cp.wait_send()
    for r in range(4):

        @pl.when(r >= blk)
        def _():
            f_copy(0, r).wait_send()
            f_copy(1, r).wait_send()

        @pl.when(r >= across_blk)
        def _():
            f_copy(2, r).wait_send()

    for r in range(2):
        for kind in range(3):
            c_copy(kind, r).wait_send()


def per_device(root, front, coupling, blocks, jci, jcv, jri, jrv, resid, noise, count):
    vmem = pl.BlockSpec(memory_space=pltpu.VMEM)
    anyspace = pl.BlockSpec(memory_space=pl.ANY)
    dma = pltpu.SemaphoreType.DMA
    f32 = jnp.float32
    sel = jnp.broadcast_to(jnp.concatenate([blocks[0], blocks[0]])[:, None], (8, 128))
    out = pl.pallas_call(
        kernel,
        out_shape=jax.ShapeDtypeStruct((1, 512), f32),
        in_specs=[vmem] + [anyspace] * 2 + [vmem] * 7 + [pl.BlockSpec(memory_space=pltpu.SMEM)],
        out_specs=vmem,
        scratch_shapes=[
            pltpu.VMEM((2, 2, 2, 2, 8, 128), f32),
            pltpu.VMEM((8, 2, TILES, 8, 128), f32),
            pltpu.VMEM((8, 2, TILES, 8, 128), f32),
            pltpu.VMEM((4, 1024, 256), f32),
            pltpu.VMEM((4, 512, 256), f32),
            pltpu.VMEM((1024, 512), f32),
            pltpu.VMEM((1024, 512), f32),
            pltpu.VMEM((640, 512), f32),
            pltpu.VMEM((512, 512), f32),
            pltpu.VMEM((4, 128, 640), f32),
            pltpu.VMEM((4, 128, 640), f32),
            pltpu.VMEM((2, 128, 640), f32),
            pltpu.VMEM((4, 8, 128), jnp.int32),
            pltpu.SMEM((4, 8, 128), jnp.int32),
            dma((2, 2, 4)), dma((9,)), dma((2, 8, 2)), dma((8, 2)), dma((8, 2)), dma((8, 2)),
            dma((4,)), dma((4,)),
            dma((3, 4)), dma((4, 4)), dma((3, 2)), dma((4, 2)),
            dma((4,)), dma((4,)), dma, dma,
        ],
        compiler_params=pltpu.CompilerParams(
            collective_id=0, has_side_effects=True, vmem_limit_bytes=48 << 20
        ),
        name="selected_inverse",
    )(
        root, front, coupling, sel, jci, jcv, jri, jrv,
        resid.reshape(1, -1), noise.reshape(1, -1), count,
    )
    return out.reshape(-1)


def solution(mesh):
    placed = (
        P("leaf", "blk"),
        P("leaf", "blk"),
        P("leaf", "blk"),
        P("leaf", None),
        P(None, ("leaf", "blk")),
        P(None, ("leaf", "blk")),
        P(None, ("leaf", "blk")),
        P(None, ("leaf", "blk")),
        P(("leaf", "blk")),
        P(("leaf", "blk")),
        P(("leaf", "blk")),
    )
    return jax.shard_map(
        per_device, mesh=mesh, in_specs=placed, out_specs=P(("leaf", "blk")), check_vma=False
    )
```

```python
import functools

import jax
import jax.numpy as jnp
from jax import lax
from jax.experimental import pallas as pl
from jax.experimental.pallas import tpu as pltpu
from jax.sharding import PartitionSpec as P

MESH = pl.DeviceIdType.MESH
TILES = 18


def split(a):
    high = a.astype(jnp.bfloat16)
    return high, (a - high.astype(jnp.float32)).astype(jnp.bfloat16)


def dot(a, b, axis=1):
    def one(p, q):
        return lax.dot_general(p, q, (((axis,), (0,)), ((), ())), preferred_element_type=jnp.float32)

    return one(a[0], b[0]) + (one(a[0], b[1]) + one(a[1], b[0]))


def kernel(
    l_hbm, f_ref, c_ref, sel_hbm, jci_hbm, jcv_hbm, jri_hbm, jrv_hbm, resid_hbm, noise_hbm, count_hbm,
    out_ref,
    l_ref, sel_ref, jci_ref, jcv_ref, jri_ref, jrv_ref, resid_ref, noise_ref, sel_own, count_ref, in_sem,
    l_buf, z_own, z_oth, f_buf, c_buf, j_high, j_low, v_high, v_low, g_buf, g_high, g_low, s_high, s_low,
    a_send, a_pass, a_recv, a_sum, sel_buf, sel_sm,
    l_send, l_recv, z_send, z_recv, d_send, d_recv, sel_send, sel_recv,
    fc_send, fc_recv, cc_send, cc_recv, x_send, x_recv, as_send, as_recv,
):
    leaf = lax.axis_index("leaf")
    blk = lax.axis_index("blk")
    ylo, x, z = lax.div(leaf, 32), lax.rem(lax.div(leaf, 8), 4), lax.rem(leaf, 8)
    yhi, core = lax.div(blk, 2), lax.rem(blk, 2)

    def device(ylo_d, x_d, z_d, blk_d):
        return {"leaf": ylo_d * 32 + x_d * 8 + z_d, "blk": blk_d}

    def copy(src, dst, send, recv, to):
        return pltpu.make_async_remote_copy(
            src_ref=src, dst_ref=dst, send_sem=send, recv_sem=recv, device_id=to, device_id_type=MESH
        )

    zr, zl = lax.rem(z + 1, 8), lax.rem(z + 7, 8)
    right, left = device(ylo, x, zr, blk), device(ylo, x, zl, blk)
    mate_blk = 2 * yhi + 1 - core
    mate = device(ylo, x, z, mate_blk)
    across_blk = 2 * (1 - yhi) + core
    across = device(ylo, x, z, across_blk)
    far_blk = 2 * (1 - yhi) + 1 - core

    loads = [
        pltpu.make_async_copy(src, dst, in_sem.at[n])
        for n, (src, dst) in enumerate(
            [
                (l_hbm, l_ref), (sel_hbm, sel_own), (jci_hbm, jci_ref), (jcv_hbm, jcv_ref), (jri_hbm, jri_ref),
                (jrv_hbm, jrv_ref), (resid_hbm, resid_ref), (noise_hbm, noise_ref), (count_hbm, count_ref),
            ]
        )
    ]
    for cp in loads:
        cp.start()

    barrier = pltpu.get_barrier_semaphore()
    mirror = 3 - x
    near = lax.rem(x + jnp.where(lax.rem(x, 2) == 0, 1, 3), 4)
    partners = [right, left, device(ylo, lax.rem(x + 2, 4), z, blk), device(ylo, near, z, blk)]
    for ylo_d in range(2):
        for blk_d in range(4):
            partners.append(device(ylo_d, mirror, z, blk_d))
    for d_ylo in range(2):
        for d_blk in range(4):
            if (d_ylo, d_blk) != (0, 0):
                partners.append(device(lax.rem(ylo + d_ylo, 2), x, z, lax.rem(blk + d_blk, 4)))
    for p in partners:
        pl.semaphore_signal(barrier, inc=1, device_id=p, device_id_type=MESH)
    loads[0].wait()
    loads[1].wait()
    row = lax.broadcasted_iota(jnp.int32, (8, 128), 0)
    choices = jnp.zeros((8, 128), jnp.int32)
    for i in range(4):
        choices = jnp.where(row == i, sel_own[0, i], choices)
    sel_ref[...] = choices
    for h in range(2):
        for core_d in range(2):
            for u in range(2):
                for q in range(2):
                    r, c = 16 * core_d + 8 * u, 256 * h + 128 * q
                    l_buf[h, core_d, u, q] = l_ref[r : r + 8, c : c + 128]
    pl.semaphore_wait(barrier, len(partners))

    upper = ylo == 0
    spread = [(h, ylo_d, blk_d) for h in range(2) for ylo_d in range(2) for blk_d in range(4)]
    x_to = jnp.where(upper, x, mirror)

    def spread_copy(h, ylo_d, blk_d):
        slot = jnp.where(upper, 0, 4 - x) + 2 * blk + h
        return (
            l_buf.at[h, blk_d % 2], z_own.at[0, :, pl.ds(2 * slot, 2)],
            l_send.at[h, ylo_d, blk_d], l_recv.at[slot], device(ylo_d, x_to, z, blk_d),
        )

    def spread_valid(h, ylo_d, blk_d):
        valid = 2 * blk + h <= jnp.where(upper, x, 4 + x)
        mine = upper & (ylo_d == ylo) & (blk_d == blk)
        return valid & jnp.logical_not(mine), valid & mine

    for key in spread:
        away, here = spread_valid(*key)

        @pl.when(away)
        def _():
            copy(*spread_copy(*key)).start()

        @pl.when(here)
        def _():
            src, dst, _, sem, _ = spread_copy(*key)
            pltpu.make_async_copy(src, dst, sem).start()

    sel_copies = []
    for d in range(1, 4):
        cp = copy(
            sel_ref, sel_buf.at[4 - d], sel_send.at[d], sel_recv.at[4 - d],
            device(ylo, lax.rem(x + d, 4), z, blk),
        )
        cp.start()
        sel_copies.append(cp)
    own_sel = pltpu.make_async_copy(sel_ref, sel_buf.at[0], sel_recv.at[0])
    own_sel.start()

    def f_rows(r):
        return pl.ds(256 * r, 256)

    def f_copy(kind, r):
        if kind == 0:
            return copy(f_ref.at[f_rows(r)], f_buf.at[blk, f_rows(r)], fc_send.at[0, r], fc_recv.at[0, r], mate)
        if kind == 1:
            return copy(f_ref.at[f_rows(r)], f_buf.at[blk, f_rows(r)], fc_send.at[1, r], fc_recv.at[1, r], across)
        return copy(
            f_buf.at[across_blk, f_rows(r)], f_buf.at[across_blk, f_rows(r)], fc_send.at[2, r], fc_recv.at[2, r], mate
        )

    def c_copy(kind, r):
        if kind == 0:
            return copy(c_ref.at[f_rows(r)], c_buf.at[blk, f_rows(r)], cc_send.at[0, r], cc_recv.at[0, r], mate)
        if kind == 1:
            return copy(c_ref.at[f_rows(r)], c_buf.at[blk, f_rows(r)], cc_send.at[1, r], cc_recv.at[1, r], across)
        return copy(
            c_buf.at[across_blk, f_rows(r)], c_buf.at[across_blk, f_rows(r)], cc_send.at[2, r], cc_recv.at[2, r], mate
        )

    f_own = [pltpu.make_async_copy(f_ref.at[f_rows(r)], f_buf.at[blk, f_rows(r)], fc_recv.at[3, r]) for r in range(4)]
    c_own = [pltpu.make_async_copy(c_ref.at[f_rows(r)], c_buf.at[blk, f_rows(r)], cc_recv.at[3, r]) for r in range(2)]

    for kind in (1, 0):
        for r in range(4):

            @pl.when(r >= blk)
            def _():
                f_copy(kind, r).start()

        for r in range(2):
            c_copy(kind, r).start()
    for r in range(4):

        @pl.when(r >= blk)
        def _():
            f_own[r].start()

    for r in range(2):
        c_own[r].start()

    for cp in loads[2:]:
        cp.wait()

    @pl.loop(0, 16)
    def _(i):
        rows = lax.broadcasted_iota(jnp.int32, (64, 512), 0) + i * 64
        acc = jnp.zeros((64, 512), jnp.float32)
        for k in range(6):
            acc = acc + jnp.where(rows == jci_ref[k : k + 1, :], jcv_ref[k : k + 1, :], 0.0)
        at = pl.ds(pl.multiple_of(i * 64, 64), 64)
        j_high[at, :], j_low[at, :] = split(acc)

    for slot in range(9):
        tile = z_own.at[0, :, pl.ds(2 * slot, 2)]
        pltpu.make_async_copy(tile, tile, l_recv.at[slot]).wait()

    def sub(ref, s, u):
        return ref.at[s, u]

    z_copies = []

    def ring(s, u, way):
        to = s + 1 if way == 0 else (s + 7) % 8
        cp = copy(sub(z_own, s, u), sub(z_own, to, u), z_send.at[way, s, u], z_recv.at[to, u], right if way == 0 else left)
        cp.start()
        z_copies.append(cp)

    def share(s, u):
        cp = copy(sub(z_own, s, u), sub(z_oth, s, u), d_send.at[s, u], d_recv.at[s, u], mate)
        cp.start()
        return cp

    shares = []

    def arrived(s, u):
        pltpu.make_async_copy(sub(z_own, s, u), sub(z_own, s, u), z_recv.at[s, u]).wait()

    for u in range(2):
        ring(0, u, 0)
        ring(0, u, 1)
        shares.append(share(0, u))
        if u == 0:
            for cp in z_copies:
                cp.wait_send()
    for s in range(1, 4):
        for u in range(2):
            arrived(s, u)
            if s < 3 or u == 0:
                ring(s, u, 0)
            shares.append(share(s, u))
            arrived(8 - s, u)
            if s < 3 or u == 1:
                ring(8 - s, u, 1)
            shares.append(share(8 - s, u))
    for u in range(2):
        arrived(4, u)
        shares.append(share(4, u))
    for cp in sel_copies:
        cp.wait()
    own_sel.wait()
    pltpu.sync_copy(sel_buf, sel_sm)
    for cp in shares:
        cp.wait()

    def gram(d):
        for i in range(4):
            j = sel_sm[d, lax.rem(i + core, 4), 0]
            choice = sel_buf[d, pl.ds(lax.rem(i + core, 4), 1), :]
            last0 = 2 * x + 1
            last1 = 15 - 2 * x
            below = 2 * (x + 1) + jnp.minimum(j, last1)
            at = slice(128 * i, 128 * i + 128)
            for n, ref in enumerate((z_own, z_oth)):
                part = ref[:, :, j].reshape(128, 128)
                s_high[256 * n : 256 * n + 128, at], s_low[256 * n : 256 * n + 128, at] = split(
                    jnp.where(choice <= last0, part, 0.0)
                )
                part = ref[:, :, below].reshape(128, 128)
                s_high[256 * n + 128 : 256 * n + 256, at], s_low[256 * n + 128 : 256 * n + 256, at] = split(
                    jnp.where(choice <= last1, part, 0.0)
                )

        def cols(a, b):
            return s_high[:, a:b], s_low[:, a:b]

        first = dot(cols(0, 128), cols(0, 384), axis=0)
        second = dot(cols(256, 384), cols(256, 512), axis=0)
        a_send[d, :, 0:128] = first[:, 0:128]
        a_send[d, :, 128:384] = 2.0 * first[:, 128:384]
        a_send[d, :, 384:512] = second[:, 0:128]
        a_send[d, :, 512:640] = 2.0 * second[:, 128:256]

    x_next = device(ylo, lax.rem(x + 1, 4), z, blk)
    x_last = device(ylo, lax.rem(x + 3, 4), z, blk)
    top, bottom = pl.ds(0, 64), pl.ds(64, 64)
    x_copies = [
        copy(a_send.at[2, top], a_pass.at[0], x_send.at[0], x_recv.at[0], x_next),
        copy(a_send.at[2, bottom], a_pass.at[1], x_send.at[1], x_recv.at[1], x_last),
        copy(a_send.at[1, bottom], a_recv.at[0, bottom], x_send.at[2], x_recv.at[2], x_next),
        copy(a_send.at[3, top], a_recv.at[1, top], x_send.at[3], x_recv.at[3], x_last),
        copy(a_send.at[1, top], a_recv.at[0, top], x_send.at[4], x_recv.at[4], x_next),
        copy(a_send.at[3, bottom], a_recv.at[1, bottom], x_send.at[5], x_recv.at[5], x_last),
    ]
    gram(2)
    x_copies[0].start()
    x_copies[1].start()
    gram(1)
    x_copies[2].start()
    gram(3)
    x_copies[3].start()
    gram(0)
    x_copies[0].wait_recv()
    a_send[1, 0:64, :] = a_send[1, 0:64, :] + a_pass[0]
    x_copies[4].start()
    x_copies[1].wait_recv()
    a_send[3, 64:128, :] = a_send[3, 64:128, :] + a_pass[1]
    x_copies[5].start()

    for r in range(4):

        @pl.when(r >= across_blk)
        def _():
            f_copy(1, r).wait_recv()
            f_copy(2, r).start()

    for r in range(2):
        c_copy(1, r).wait_recv()
        c_copy(2, r).start()
    for r in range(4):

        @pl.when(r >= blk)
        def _():
            f_own[r].wait()

        @pl.when(r >= mate_blk)
        def _():
            f_copy(0, r).wait_recv()

        @pl.when(r >= far_blk)
        def _():
            f_copy(2, r).wait_recv()

    square = jnp.zeros((1, 512), jnp.float32)
    for r in range(4):
        rows = slice(256 * r, 256 * r + 256)
        acc = jnp.zeros((256, 512), jnp.float32)
        for s in range(r + 1):
            at = slice(256 * s, 256 * s + 256)
            acc = acc + dot(split(f_buf[s, rows, :]), (j_high[at, :], j_low[at, :]))
        v_high[rows, :], v_low[rows, :] = split(acc)
        square = square + jnp.sum(acc * acc, axis=0, keepdims=True)

    for r in range(2):
        c_own[r].wait()
        c_copy(0, r).wait_recv()
        c_copy(2, r).wait_recv()
    for q in range(4):
        rows = lax.broadcasted_iota(jnp.int32, (128, 512), 0) + q * 128
        root = jnp.zeros((128, 512), jnp.float32)
        for k in range(2):
            root = root + jnp.where(rows == jri_ref[k : k + 1, :], jrv_ref[k : k + 1, :], 0.0)
        acc = -root
        for s in range(4):
            at = slice(256 * s, 256 * s + 256)
            acc = acc + dot(split(c_buf[s, 128 * q : 128 * q + 128, :]), (v_high[at, :], v_low[at, :]))
        at = slice(128 * q, 128 * q + 128)
        g_buf[at, :] = acc
        g_high[at, :], g_low[at, :] = split(acc)
        if q == 0:
            g_buf[512:640, :] = acc
            g_high[512:640, :], g_low[512:640, :] = split(acc)

    for cp in x_copies[2:]:
        cp.wait_recv()
    a_sum[0] = a_send[0] + a_recv[0] + a_recv[1]
    a_share = copy(a_sum.at[0], a_sum.at[1], as_send, as_recv, mate)
    a_share.start()

    def quad(n, c):
        total = jnp.zeros((1, 512), jnp.float32)
        for a, b, off in ((0, 384, 0), (384, 640, 256)):
            start = pl.multiple_of(c * 128 + off, 128)
            at = pl.ds(start, b - a)
            w = dot(split(a_sum[n, :, a:b]), (g_high[at, :], g_low[at, :]))
            total = total + jnp.sum(w * g_buf[pl.ds(start, 128), :], axis=0, keepdims=True)
        return total

    omega = noise_ref[...] + square + quad(0, core)
    a_share.wait()
    omega = omega + quad(1, 1 - core)
    live = lax.broadcasted_iota(jnp.int32, (1, 512), 1) < count_ref[0]
    out_ref[...] = jnp.where(live, resid_ref[...] / jnp.sqrt(omega), 0.0)

    for key in spread:

        @pl.when(spread_valid(*key)[0])
        def _():
            copy(*spread_copy(*key)).wait_send()

    for cp in z_copies[2:]:
        cp.wait_send()
    for cp in x_copies:
        cp.wait_send()
    for r in range(4):

        @pl.when(r >= blk)
        def _():
            f_copy(0, r).wait_send()
            f_copy(1, r).wait_send()

        @pl.when(r >= across_blk)
        def _():
            f_copy(2, r).wait_send()

    for r in range(2):
        for kind in range(3):
            c_copy(kind, r).wait_send()


def per_device(root, front, coupling, blocks, jci, jcv, jri, jrv, resid, noise, count):
    vmem = pl.BlockSpec(memory_space=pltpu.VMEM)
    dma = pltpu.SemaphoreType.DMA
    f32, bf16 = jnp.float32, jnp.bfloat16
    out = pl.pallas_call(
        kernel,
        out_shape=jax.ShapeDtypeStruct((1, 512), f32),
        in_specs=[pl.BlockSpec(memory_space=pltpu.HBM)] * 11,
        out_specs=vmem,
        scratch_shapes=[
            pltpu.VMEM((32, 512), f32),
            pltpu.VMEM((8, 128), jnp.int32),
            pltpu.VMEM((6, 512), jnp.int32),
            pltpu.VMEM((6, 512), f32),
            pltpu.VMEM((2, 512), jnp.int32),
            pltpu.VMEM((2, 512), f32),
            pltpu.VMEM((1, 512), f32),
            pltpu.VMEM((1, 512), f32),
            pltpu.SMEM((1, 4), jnp.int32),
            pltpu.SMEM((1,), jnp.int32),
            dma((9,)),
            pltpu.VMEM((2, 2, 2, 2, 8, 128), f32),
            pltpu.VMEM((8, 2, TILES, 8, 128), f32),
            pltpu.VMEM((8, 2, TILES, 8, 128), f32),
            pltpu.VMEM((4, 1024, 256), f32),
            pltpu.VMEM((4, 512, 256), f32),
            pltpu.VMEM((1024, 512), bf16),
            pltpu.VMEM((1024, 512), bf16),
            pltpu.VMEM((1024, 512), bf16),
            pltpu.VMEM((1024, 512), bf16),
            pltpu.VMEM((640, 512), f32),
            pltpu.VMEM((640, 512), bf16),
            pltpu.VMEM((640, 512), bf16),
            pltpu.VMEM((512, 512), bf16),
            pltpu.VMEM((512, 512), bf16),
            pltpu.VMEM((4, 128, 640), f32),
            pltpu.VMEM((2, 64, 640), f32),
            pltpu.VMEM((2, 128, 640), f32),
            pltpu.VMEM((2, 128, 640), f32),
            pltpu.VMEM((4, 8, 128), jnp.int32),
            pltpu.SMEM((4, 8, 128), jnp.int32),
            dma((2, 2, 4)), dma((9,)), dma((2, 8, 2)), dma((8, 2)), dma((8, 2)), dma((8, 2)),
            dma((4,)), dma((4,)),
            dma((3, 4)), dma((4, 4)), dma((3, 2)), dma((4, 2)),
            dma((6,)), dma((6,)), dma, dma,
        ],
        compiler_params=pltpu.CompilerParams(
            collective_id=0, has_side_effects=True, vmem_limit_bytes=63 << 20
        ),
        name="selected_inverse",
    )(
        root, front, coupling, blocks, jci, jcv, jri, jrv,
        resid.reshape(1, -1), noise.reshape(1, -1), count,
    )
    return out.reshape(-1)


def solution(mesh):
    placed = (
        P("leaf", "blk"),
        P("leaf", "blk"),
        P("leaf", "blk"),
        P("leaf", None),
        P(None, ("leaf", "blk")),
        P(None, ("leaf", "blk")),
        P(None, ("leaf", "blk")),
        P(None, ("leaf", "blk")),
        P(("leaf", "blk")),
        P(("leaf", "blk")),
        P(("leaf", "blk")),
    )
    return jax.shard_map(
        per_device, mesh=mesh, in_specs=placed, out_specs=P(("leaf", "blk")), check_vma=False
    )
```

```python
import functools

import jax
import jax.numpy as jnp
from jax import lax
from jax.experimental import pallas as pl
from jax.experimental.pallas import tpu as pltpu
from jax.sharding import PartitionSpec as P

MESH = pl.DeviceIdType.MESH
TILES = 18


def split(a):
    high = a.astype(jnp.bfloat16)
    return high, (a - high.astype(jnp.float32)).astype(jnp.bfloat16)


def dot(a, b, axis=1):
    def one(p, q):
        return lax.dot_general(p, q, (((axis,), (0,)), ((), ())), preferred_element_type=jnp.float32)

    return one(a[0], b[0]) + (one(a[0], b[1]) + one(a[1], b[0]))


def kernel(
    l_hbm, f_ref, c_ref, sel_hbm, jci_hbm, jcv_hbm, jri_hbm, jrv_hbm, resid_hbm, noise_hbm, count_hbm,
    out_ref,
    l_ref, sel_ref, jci_ref, jcv_ref, jri_ref, jrv_ref, resid_ref, noise_ref, sel_own, count_ref, in_sem,
    l_buf, z_own, z_oth, f_buf, c_buf, j_high, j_low, v_high, v_low, g_buf, g_high, g_low, s_high, s_low,
    a_send, a_pass, a_recv, a_sum, sel_buf, sel_sm,
    l_send, l_recv, z_send, z_recv, d_send, d_recv, sel_send, sel_recv,
    fc_send, fc_recv, cc_send, cc_recv, x_send, x_recv, as_send, as_recv,
):
    leaf = lax.axis_index("leaf")
    blk = lax.axis_index("blk")
    ylo, x, z = lax.div(leaf, 32), lax.rem(lax.div(leaf, 8), 4), lax.rem(leaf, 8)
    yhi, core = lax.div(blk, 2), lax.rem(blk, 2)

    def device(ylo_d, x_d, z_d, blk_d):
        return {"leaf": ylo_d * 32 + x_d * 8 + z_d, "blk": blk_d}

    def copy(src, dst, send, recv, to):
        return pltpu.make_async_remote_copy(
            src_ref=src, dst_ref=dst, send_sem=send, recv_sem=recv, device_id=to, device_id_type=MESH
        )

    zr, zl = lax.rem(z + 1, 8), lax.rem(z + 7, 8)
    right, left = device(ylo, x, zr, blk), device(ylo, x, zl, blk)
    mate_blk = 2 * yhi + 1 - core
    mate = device(ylo, x, z, mate_blk)
    across_blk = 2 * (1 - yhi) + core
    across = device(ylo, x, z, across_blk)
    far_blk = 2 * (1 - yhi) + 1 - core

    loads = [
        pltpu.make_async_copy(src, dst, in_sem.at[n])
        for n, (src, dst) in enumerate(
            [
                (l_hbm, l_ref), (sel_hbm, sel_own), (jci_hbm, jci_ref), (jcv_hbm, jcv_ref), (jri_hbm, jri_ref),
                (jrv_hbm, jrv_ref), (resid_hbm, resid_ref), (noise_hbm, noise_ref), (count_hbm, count_ref),
            ]
        )
    ]
    for cp in loads:
        cp.start()

    a_send[:, 128:136, :] = jnp.zeros((4, 8, 512), jnp.float32)

    barrier = pltpu.get_barrier_semaphore()
    mirror = 3 - x
    near = lax.rem(x + jnp.where(lax.rem(x, 2) == 0, 1, 3), 4)
    partners = [right, left, device(ylo, lax.rem(x + 2, 4), z, blk), device(ylo, near, z, blk)]
    for ylo_d in range(2):
        for blk_d in range(4):
            partners.append(device(ylo_d, mirror, z, blk_d))
    for d_ylo in range(2):
        for d_blk in range(4):
            if (d_ylo, d_blk) != (0, 0):
                partners.append(device(lax.rem(ylo + d_ylo, 2), x, z, lax.rem(blk + d_blk, 4)))
    for p in partners:
        pl.semaphore_signal(barrier, inc=1, device_id=p, device_id_type=MESH)
    loads[0].wait()
    loads[1].wait()
    row = lax.broadcasted_iota(jnp.int32, (8, 128), 0)
    choices = jnp.zeros((8, 128), jnp.int32)
    for i in range(4):
        choices = jnp.where(row == i, sel_own[0, i], choices)
    sel_ref[...] = choices
    for h in range(2):
        for core_d in range(2):
            for u in range(2):
                for q in range(2):
                    r, c = 16 * core_d + 8 * u, 256 * h + 128 * q
                    l_buf[h, core_d, u, q] = l_ref[r : r + 8, c : c + 128]
    pl.semaphore_wait(barrier, len(partners))

    upper = ylo == 0
    spread = [(h, ylo_d, blk_d) for h in range(2) for ylo_d in range(2) for blk_d in range(4)]
    x_to = jnp.where(upper, x, mirror)

    def spread_copy(h, ylo_d, blk_d):
        slot = jnp.where(upper, 0, 4 - x) + 2 * blk + h
        return (
            l_buf.at[h, blk_d % 2], z_own.at[0, :, pl.ds(2 * slot, 2)],
            l_send.at[h, ylo_d, blk_d], l_recv.at[slot], device(ylo_d, x_to, z, blk_d),
        )

    def spread_valid(h, ylo_d, blk_d):
        valid = 2 * blk + h <= jnp.where(upper, x, 4 + x)
        mine = upper & (ylo_d == ylo) & (blk_d == blk)
        return valid & jnp.logical_not(mine), valid & mine

    for key in spread:
        away, here = spread_valid(*key)

        @pl.when(away)
        def _():
            copy(*spread_copy(*key)).start()

        @pl.when(here)
        def _():
            src, dst, _, sem, _ = spread_copy(*key)
            pltpu.make_async_copy(src, dst, sem).start()

    sel_copies = []
    for d in range(1, 4):
        cp = copy(
            sel_ref, sel_buf.at[4 - d], sel_send.at[d], sel_recv.at[4 - d],
            device(ylo, lax.rem(x + d, 4), z, blk),
        )
        cp.start()
        sel_copies.append(cp)
    own_sel = pltpu.make_async_copy(sel_ref, sel_buf.at[0], sel_recv.at[0])
    own_sel.start()

    def f_rows(r):
        return pl.ds(256 * r, 256)

    def f_copy(kind, r):
        if kind == 0:
            return copy(f_ref.at[f_rows(r)], f_buf.at[blk, f_rows(r)], fc_send.at[0, r], fc_recv.at[0, r], mate)
        if kind == 1:
            return copy(f_ref.at[f_rows(r)], f_buf.at[blk, f_rows(r)], fc_send.at[1, r], fc_recv.at[1, r], across)
        return copy(
            f_buf.at[across_blk, f_rows(r)], f_buf.at[across_blk, f_rows(r)], fc_send.at[2, r], fc_recv.at[2, r], mate
        )

    def c_copy(kind, r):
        if kind == 0:
            return copy(c_ref.at[f_rows(r)], c_buf.at[blk, f_rows(r)], cc_send.at[0, r], cc_recv.at[0, r], mate)
        if kind == 1:
            return copy(c_ref.at[f_rows(r)], c_buf.at[blk, f_rows(r)], cc_send.at[1, r], cc_recv.at[1, r], across)
        return copy(
            c_buf.at[across_blk, f_rows(r)], c_buf.at[across_blk, f_rows(r)], cc_send.at[2, r], cc_recv.at[2, r], mate
        )

    f_own = [pltpu.make_async_copy(f_ref.at[f_rows(r)], f_buf.at[blk, f_rows(r)], fc_recv.at[3, r]) for r in range(4)]
    c_own = [pltpu.make_async_copy(c_ref.at[f_rows(r)], c_buf.at[blk, f_rows(r)], cc_recv.at[3, r]) for r in range(2)]

    for kind in (1, 0):
        for r in range(4):

            @pl.when(r >= blk)
            def _():
                f_copy(kind, r).start()

        for r in range(2):
            c_copy(kind, r).start()
    for r in range(4):

        @pl.when(r >= blk)
        def _():
            f_own[r].start()

    for r in range(2):
        c_own[r].start()

    for cp in loads[2:]:
        cp.wait()

    @pl.loop(0, 16)
    def _(i):
        rows = lax.broadcasted_iota(jnp.int32, (64, 512), 0) + i * 64
        acc = jnp.zeros((64, 512), jnp.float32)
        for k in range(6):
            acc = acc + jnp.where(rows == jci_ref[k : k + 1, :], jcv_ref[k : k + 1, :], 0.0)
        at = pl.ds(pl.multiple_of(i * 64, 64), 64)
        j_high[at, :], j_low[at, :] = split(acc)

    for slot in range(9):
        tile = z_own.at[0, :, pl.ds(2 * slot, 2)]
        pltpu.make_async_copy(tile, tile, l_recv.at[slot]).wait()

    def sub(ref, s, u):
        return ref.at[s, u // 2, pl.ds(9 * (u % 2), 9)]

    z_copies = []

    def ring(s, u, way):
        to = s + 1 if way == 0 else (s + 7) % 8
        cp = copy(sub(z_own, s, u), sub(z_own, to, u), z_send.at[way, s, u], z_recv.at[to, u], right if way == 0 else left)
        cp.start()
        z_copies.append(cp)

    def share(s, u):
        cp = copy(sub(z_own, s, u), sub(z_oth, s, u), d_send.at[s, u], d_recv.at[s, u], mate)
        cp.start()
        return cp

    shares = []

    def arrived(s, u):
        pltpu.make_async_copy(sub(z_own, s, u), sub(z_own, s, u), z_recv.at[s, u]).wait()

    for u in range(4):
        ring(0, u, 0)
        ring(0, 3 - u, 1)
    for u in range(4):
        shares.append(share(0, u))
    for s in range(1, 4):
        for u in range(4):
            arrived(s, u)
            if s < 3 or u < 2:
                ring(s, u, 0)
            shares.append(share(s, u))
            w = 3 - u
            arrived(8 - s, w)
            if s < 3 or w >= 2:
                ring(8 - s, w, 1)
            shares.append(share(8 - s, w))
    for u in (0, 3, 1, 2):
        arrived(4, u)
        shares.append(share(4, u))
    for cp in sel_copies:
        cp.wait()
    own_sel.wait()
    pltpu.sync_copy(sel_buf, sel_sm)
    for cp in shares:
        cp.wait()

    row_is = lax.broadcasted_iota(jnp.int32, (128, 128), 0)
    col_is = lax.broadcasted_iota(jnp.int32, (128, 128), 1)

    def gram(d):
        for i in range(4):
            j = sel_sm[d, lax.rem(i + core, 4), 0]
            choice = sel_buf[d, pl.ds(lax.rem(i + core, 4), 1), :]
            last0 = 2 * x + 1
            last1 = 15 - 2 * x
            below = 2 * (x + 1) + jnp.minimum(j, last1)
            at = slice(128 * i, 128 * i + 128)
            for n, ref in enumerate((z_own, z_oth)):
                part = ref[:, :, j].reshape(128, 128)
                s_high[256 * n : 256 * n + 128, at], s_low[256 * n : 256 * n + 128, at] = split(
                    jnp.where(choice <= last0, part, 0.0)
                )
                part = ref[:, :, below].reshape(128, 128)
                s_high[256 * n + 128 : 256 * n + 256, at], s_low[256 * n + 128 : 256 * n + 256, at] = split(
                    jnp.where(choice <= last1, part, 0.0)
                )

        def cols(a, b):
            return s_high[:, a:b], s_low[:, a:b]

        first = dot(cols(0, 128), cols(0, 384), axis=0)
        second = dot(cols(256, 384), cols(256, 512), axis=0)
        a_send[d, 0:128, 0:128] = jnp.where(
            row_is > col_is, 2.0 * first[:, 0:128], jnp.where(row_is == col_is, first[:, 0:128], 2.0 * second[:, 0:128])
        )
        a_send[d, 128:136, 0:128] = jnp.broadcast_to(
            jnp.sum(jnp.where(row_is == col_is, second[:, 0:128], 0.0), axis=0, keepdims=True), (8, 128)
        )
        a_send[d, 0:128, 128:384] = 2.0 * first[:, 128:384]
        a_send[d, 0:128, 384:512] = 2.0 * second[:, 128:256]

    x_next = device(ylo, lax.rem(x + 1, 4), z, blk)
    x_last = device(ylo, lax.rem(x + 3, 4), z, blk)
    top, bottom = pl.ds(0, 64), pl.ds(64, 72)
    x_copies = [
        copy(a_send.at[2, top], a_pass.at[pl.ds(0, 64)], x_send.at[0], x_recv.at[0], x_next),
        copy(a_send.at[2, bottom], a_pass.at[pl.ds(64, 72)], x_send.at[1], x_recv.at[1], x_last),
        copy(a_send.at[1, bottom], a_recv.at[0, bottom], x_send.at[2], x_recv.at[2], x_next),
        copy(a_send.at[3, top], a_recv.at[1, top], x_send.at[3], x_recv.at[3], x_last),
        copy(a_send.at[1, top], a_recv.at[0, top], x_send.at[4], x_recv.at[4], x_next),
        copy(a_send.at[3, bottom], a_recv.at[1, bottom], x_send.at[5], x_recv.at[5], x_last),
    ]
    gram(2)
    x_copies[0].start()
    x_copies[1].start()
    gram(1)
    x_copies[2].start()
    gram(3)
    x_copies[3].start()
    gram(0)
    x_copies[0].wait_recv()
    a_send[1, 0:64, :] = a_send[1, 0:64, :] + a_pass[0:64, :]
    x_copies[4].start()
    x_copies[1].wait_recv()
    a_send[3, 64:136, :] = a_send[3, 64:136, :] + a_pass[64:136, :]
    x_copies[5].start()

    for r in range(4):

        @pl.when(r >= across_blk)
        def _():
            f_copy(1, r).wait_recv()
            f_copy(2, r).start()

    for r in range(2):
        c_copy(1, r).wait_recv()
        c_copy(2, r).start()
    for r in range(4):

        @pl.when(r >= blk)
        def _():
            f_own[r].wait()

        @pl.when(r >= mate_blk)
        def _():
            f_copy(0, r).wait_recv()

        @pl.when(r >= far_blk)
        def _():
            f_copy(2, r).wait_recv()

    square = jnp.zeros((1, 512), jnp.float32)
    for r in range(4):
        rows = slice(256 * r, 256 * r + 256)
        acc = jnp.zeros((256, 512), jnp.float32)
        for s in range(r + 1):
            at = slice(256 * s, 256 * s + 256)
            acc = acc + dot(split(f_buf[s, rows, :]), (j_high[at, :], j_low[at, :]))
        v_high[rows, :], v_low[rows, :] = split(acc)
        square = square + jnp.sum(acc * acc, axis=0, keepdims=True)

    for r in range(2):
        c_own[r].wait()
        c_copy(0, r).wait_recv()
        c_copy(2, r).wait_recv()
    for q in range(4):
        rows = lax.broadcasted_iota(jnp.int32, (128, 512), 0) + q * 128
        root = jnp.zeros((128, 512), jnp.float32)
        for k in range(2):
            root = root + jnp.where(rows == jri_ref[k : k + 1, :], jrv_ref[k : k + 1, :], 0.0)
        acc = -root
        for s in range(4):
            at = slice(256 * s, 256 * s + 256)
            acc = acc + dot(split(c_buf[s, 128 * q : 128 * q + 128, :]), (v_high[at, :], v_low[at, :]))
        at = slice(128 * q, 128 * q + 128)
        g_buf[at, :] = acc
        g_high[at, :], g_low[at, :] = split(acc)
        if q == 0:
            g_buf[512:640, :] = acc
            g_high[512:640, :], g_low[512:640, :] = split(acc)

    for cp in x_copies[2:]:
        cp.wait_recv()
    a_sum[0] = a_send[0] + a_recv[0] + a_recv[1]
    a_share = copy(a_sum.at[0], a_sum.at[1], as_send, as_recv, mate)
    a_share.start()

    def quad(n, c):
        both = a_sum[n, 0:128, 0:128]
        lower = jnp.where(row_is >= col_is, both, 0.0)
        diagonal = jnp.where(row_is == col_is, a_sum[n, 128:129, 0:128], 0.0)
        upper_ = jnp.where(row_is < col_is, both, diagonal)
        total = jnp.zeros((1, 512), jnp.float32)
        for corner, a, b, off in ((lower, 128, 384, 0), (upper_, 384, 512, 256)):
            start = pl.multiple_of(c * 128 + off, 128)
            near_ = pl.ds(start, 128)
            after = pl.ds(pl.multiple_of(start + 128, 128), b - a)
            w = dot(split(corner), (g_high[near_, :], g_low[near_, :]))
            w = w + dot(split(a_sum[n, 0:128, a:b]), (g_high[after, :], g_low[after, :]))
            total = total + jnp.sum(w * g_buf[near_, :], axis=0, keepdims=True)
        return total

    omega = noise_ref[...] + square + quad(0, core)
    a_share.wait()
    omega = omega + quad(1, 1 - core)
    live = lax.broadcasted_iota(jnp.int32, (1, 512), 1) < count_ref[0]
    out_ref[...] = jnp.where(live, resid_ref[...] / jnp.sqrt(omega), 0.0)

    for key in spread:

        @pl.when(spread_valid(*key)[0])
        def _():
            copy(*spread_copy(*key)).wait_send()

    for cp in z_copies:
        cp.wait_send()
    for cp in x_copies:
        cp.wait_send()
    for r in range(4):

        @pl.when(r >= blk)
        def _():
            f_copy(0, r).wait_send()
            f_copy(1, r).wait_send()

        @pl.when(r >= across_blk)
        def _():
            f_copy(2, r).wait_send()

    for r in range(2):
        for kind in range(3):
            c_copy(kind, r).wait_send()


def per_device(root, front, coupling, blocks, jci, jcv, jri, jrv, resid, noise, count):
    vmem = pl.BlockSpec(memory_space=pltpu.VMEM)
    dma = pltpu.SemaphoreType.DMA
    f32, bf16 = jnp.float32, jnp.bfloat16
    out = pl.pallas_call(
        kernel,
        out_shape=jax.ShapeDtypeStruct((1, 512), f32),
        in_specs=[pl.BlockSpec(memory_space=pltpu.HBM)] * 11,
        out_specs=vmem,
        scratch_shapes=[
            pltpu.VMEM((32, 512), f32),
            pltpu.VMEM((8, 128), jnp.int32),
            pltpu.VMEM((6, 512), jnp.int32),
            pltpu.VMEM((6, 512), f32),
            pltpu.VMEM((2, 512), jnp.int32),
            pltpu.VMEM((2, 512), f32),
            pltpu.VMEM((1, 512), f32),
            pltpu.VMEM((1, 512), f32),
            pltpu.SMEM((1, 4), jnp.int32),
            pltpu.SMEM((1,), jnp.int32),
            dma((9,)),
            pltpu.VMEM((2, 2, 2, 2, 8, 128), f32),
            pltpu.VMEM((8, 2, TILES, 8, 128), f32),
            pltpu.VMEM((8, 2, TILES, 8, 128), f32),
            pltpu.VMEM((4, 1024, 256), f32),
            pltpu.VMEM((4, 512, 256), f32),
            pltpu.VMEM((1024, 512), bf16),
            pltpu.VMEM((1024, 512), bf16),
            pltpu.VMEM((1024, 512), bf16),
            pltpu.VMEM((1024, 512), bf16),
            pltpu.VMEM((640, 512), f32),
            pltpu.VMEM((640, 512), bf16),
            pltpu.VMEM((640, 512), bf16),
            pltpu.VMEM((512, 512), bf16),
            pltpu.VMEM((512, 512), bf16),
            pltpu.VMEM((4, 136, 512), f32),
            pltpu.VMEM((136, 512), f32),
            pltpu.VMEM((2, 136, 512), f32),
            pltpu.VMEM((2, 136, 512), f32),
            pltpu.VMEM((4, 8, 128), jnp.int32),
            pltpu.SMEM((4, 8, 128), jnp.int32),
            dma((2, 2, 4)), dma((9,)), dma((2, 8, 4)), dma((8, 4)), dma((8, 4)), dma((8, 4)),
            dma((4,)), dma((4,)),
            dma((3, 4)), dma((4, 4)), dma((3, 2)), dma((4, 2)),
            dma((6,)), dma((6,)), dma, dma,
        ],
        compiler_params=pltpu.CompilerParams(
            collective_id=0, has_side_effects=True, vmem_limit_bytes=63 << 20
        ),
        name="selected_inverse",
    )(
        root, front, coupling, blocks, jci, jcv, jri, jrv,
        resid.reshape(1, -1), noise.reshape(1, -1), count,
    )
    return out.reshape(-1)


def solution(mesh):
    placed = (
        P("leaf", "blk"),
        P("leaf", "blk"),
        P("leaf", "blk"),
        P("leaf", None),
        P(None, ("leaf", "blk")),
        P(None, ("leaf", "blk")),
        P(None, ("leaf", "blk")),
        P(None, ("leaf", "blk")),
        P(("leaf", "blk")),
        P(("leaf", "blk")),
        P(("leaf", "blk")),
    )
    return jax.shard_map(
        per_device, mesh=mesh, in_specs=placed, out_specs=P(("leaf", "blk")), check_vma=False
    )
```

```python
import functools

import jax
import jax.numpy as jnp
from jax import lax
from jax.experimental import pallas as pl
from jax.experimental.pallas import tpu as pltpu
from jax.sharding import PartitionSpec as P

MESH = pl.DeviceIdType.MESH
CROSS_AT = 2
PIECES = 4
TILES = 18


def split(a):
    high = a.astype(jnp.bfloat16)
    return high, (a - high.astype(jnp.float32)).astype(jnp.bfloat16)


def dot(a, b, axis=1):
    def one(p, q):
        return lax.dot_general(p, q, (((axis,), (0,)), ((), ())), preferred_element_type=jnp.float32)

    return one(a[0], b[0]) + (one(a[0], b[1]) + one(a[1], b[0]))


def kernel(
    l_hbm, f_ref, c_ref, sel_hbm, jci_hbm, jcv_hbm, jri_hbm, jrv_hbm, resid_hbm, noise_hbm, count_hbm,
    out_ref,
    l_ref, sel_ref, jci_ref, jcv_ref, jri_ref, jrv_ref, resid_ref, noise_ref, sel_own, count_ref, in_sem,
    l_buf, z_own, z_oth, f_buf, c_buf, j_high, j_low, v_high, v_low, g_buf, g_high, g_low, s_high, s_low,
    a_send, a_pass, a_recv, a_sum, sel_buf, sel_sm,
    l_send, l_recv, z_send, z_recv, d_send, d_recv, sel_send, sel_recv,
    fc_send, fc_recv, cc_send, cc_recv, x_send, x_recv, as_send, as_recv,
):
    leaf = lax.axis_index("leaf")
    blk = lax.axis_index("blk")
    ylo, x, z = lax.div(leaf, 32), lax.rem(lax.div(leaf, 8), 4), lax.rem(leaf, 8)
    yhi, core = lax.div(blk, 2), lax.rem(blk, 2)

    def device(ylo_d, x_d, z_d, blk_d):
        return {"leaf": ylo_d * 32 + x_d * 8 + z_d, "blk": blk_d}

    def copy(src, dst, send, recv, to):
        return pltpu.make_async_remote_copy(
            src_ref=src, dst_ref=dst, send_sem=send, recv_sem=recv, device_id=to, device_id_type=MESH
        )

    zr, zl = lax.rem(z + 1, 8), lax.rem(z + 7, 8)
    right, left = device(ylo, x, zr, blk), device(ylo, x, zl, blk)
    mate_blk = 2 * yhi + 1 - core
    mate = device(ylo, x, z, mate_blk)
    across_blk = 2 * (1 - yhi) + core
    across = device(ylo, x, z, across_blk)
    far_blk = 2 * (1 - yhi) + 1 - core

    loads = [
        pltpu.make_async_copy(src, dst, in_sem.at[n])
        for n, (src, dst) in enumerate(
            [
                (l_hbm, l_ref), (sel_hbm, sel_own), (jci_hbm, jci_ref), (jcv_hbm, jcv_ref), (jri_hbm, jri_ref),
                (jrv_hbm, jrv_ref), (resid_hbm, resid_ref), (noise_hbm, noise_ref), (count_hbm, count_ref),
            ]
        )
    ]
    loads[0].start()
    a_send[:, 128:136, :] = jnp.zeros((4, 8, 512), jnp.float32)

    barrier = pltpu.get_barrier_semaphore()
    mirror = 3 - x
    near = lax.rem(x + jnp.where(lax.rem(x, 2) == 0, 1, 3), 4)
    partners = [right, left, device(ylo, lax.rem(x + 2, 4), z, blk), device(ylo, near, z, blk)]
    for ylo_d in range(2):
        for blk_d in range(4):
            partners.append(device(ylo_d, mirror, z, blk_d))
    for d_ylo in range(2):
        for d_blk in range(4):
            if (d_ylo, d_blk) != (0, 0):
                partners.append(device(lax.rem(ylo + d_ylo, 2), x, z, lax.rem(blk + d_blk, 4)))
    for p in partners:
        pl.semaphore_signal(barrier, inc=1, device_id=p, device_id_type=MESH)
    for cp in loads[1:]:
        cp.start()
    loads[0].wait()
    for h in range(2):
        for core_d in range(2):
            for u in range(2):
                for q in range(2):
                    r, c = 16 * core_d + 8 * u, 256 * h + 128 * q
                    l_buf[core_d, u, 2 * h + q] = l_ref[r : r + 8, c : c + 128]
    pl.semaphore_wait(barrier, len(partners))

    upper = ylo == 0
    spread = [(ylo_d, blk_d) for ylo_d in range(2) for blk_d in range(4)]
    x_to = jnp.where(upper, x, mirror)
    slot_to = jnp.where(upper, 0, 4 - x) + 2 * blk
    tiles_out = jnp.clip(jnp.where(upper, x, 4 + x) + 1 - 2 * blk, 0, 2)

    def spread_copy(n, ylo_d, blk_d):
        return (
            l_buf.at[blk_d % 2, :, pl.ds(0, 2 * n)], z_own.at[0, :, pl.ds(2 * slot_to, 2 * n)],
            l_send.at[ylo_d, blk_d], l_recv.at[jnp.where(upper, blk, 2 + blk)], device(ylo_d, x_to, z, blk_d),
        )

    def spread_mine(ylo_d, blk_d):
        return upper & (ylo_d == ylo) & (blk_d == blk)

    for n in (1, 2):

        @pl.when(tiles_out == n)
        def _():
            for key in spread:
                mine = spread_mine(*key)

                @pl.when(jnp.logical_not(mine))
                def _():
                    copy(*spread_copy(n, *key)).start()

                @pl.when(mine)
                def _():
                    src, dst, _, sem, _ = spread_copy(n, *key)
                    pltpu.make_async_copy(src, dst, sem).start()

    loads[1].wait()
    row = lax.broadcasted_iota(jnp.int32, (8, 128), 0)
    choices = jnp.zeros((8, 128), jnp.int32)
    for i in range(4):
        choices = jnp.where(row == i, sel_own[0, i], choices)
    sel_ref[...] = choices
    sel_copies = []
    for d in range(1, 4):
        cp = copy(
            sel_ref, sel_buf.at[4 - d], sel_send.at[d], sel_recv.at[4 - d],
            device(ylo, lax.rem(x + d, 4), z, blk),
        )
        cp.start()
        sel_copies.append(cp)
    own_sel = pltpu.make_async_copy(sel_ref, sel_buf.at[0], sel_recv.at[0])
    own_sel.start()

    def f_rows(r):
        return pl.ds(256 * r, 256)

    def f_copy(kind, r):
        if kind == 0:
            return copy(f_ref.at[f_rows(r)], f_buf.at[blk, f_rows(r)], fc_send.at[0, r], fc_recv.at[0, r], mate)
        if kind == 1:
            return copy(f_ref.at[f_rows(r)], f_buf.at[blk, f_rows(r)], fc_send.at[1, r], fc_recv.at[1, r], across)
        return copy(
            f_buf.at[across_blk, f_rows(r)], f_buf.at[across_blk, f_rows(r)], fc_send.at[2, r], fc_recv.at[2, r], mate
        )

    def c_copy(kind, r):
        if kind == 0:
            return copy(c_ref.at[f_rows(r)], c_buf.at[blk, f_rows(r)], cc_send.at[0, r], cc_recv.at[0, r], mate)
        if kind == 1:
            return copy(c_ref.at[f_rows(r)], c_buf.at[blk, f_rows(r)], cc_send.at[1, r], cc_recv.at[1, r], across)
        return copy(
            c_buf.at[across_blk, f_rows(r)], c_buf.at[across_blk, f_rows(r)], cc_send.at[2, r], cc_recv.at[2, r], mate
        )

    f_own = [pltpu.make_async_copy(f_ref.at[f_rows(r)], f_buf.at[blk, f_rows(r)], fc_recv.at[3, r]) for r in range(4)]
    c_own = [pltpu.make_async_copy(c_ref.at[f_rows(r)], c_buf.at[blk, f_rows(r)], cc_recv.at[3, r]) for r in range(2)]

    for kind in (1, 0):
        for r in range(4):

            @pl.when(r >= blk)
            def _():
                f_copy(kind, r).start()

    for r in range(4):

        @pl.when(r >= blk)
        def _():
            f_own[r].start()

    for r in range(2):
        c_copy(0, r).start()
        c_own[r].start()

    for cp in loads[2:]:
        cp.wait()

    @pl.loop(0, 16)
    def _(i):
        rows = lax.broadcasted_iota(jnp.int32, (64, 512), 0) + i * 64
        acc = jnp.zeros((64, 512), jnp.float32)
        for k in range(6):
            acc = acc + jnp.where(rows == jci_ref[k : k + 1, :], jcv_ref[k : k + 1, :], 0.0)
        at = pl.ds(pl.multiple_of(i * 64, 64), 64)
        j_high[at, :], j_low[at, :] = split(acc)

    for source in range(6):
        half, b = source // 2 > 0, source if source < 2 else source - 2
        tiles_in = jnp.clip((7 - x if half else x) + 1 - 2 * b, 0, 2)
        first = (x + 1 if half else 0) + 2 * b
        for n in (1, 2):

            @pl.when(tiles_in == n)
            def _():
                area = z_own.at[0, :, pl.ds(2 * first, 2 * n)]
                pltpu.make_async_copy(area, area, l_recv.at[source]).wait()

    def sub(ref, s, u):
        return ref.at[s, u // (PIECES // 2), pl.ds(u % (PIECES // 2) * (2 * TILES // PIECES), 2 * TILES // PIECES)]

    z_copies = []

    def ring(s, u, way):
        to = s + 1 if way == 0 else (s + 7) % 8
        cp = copy(sub(z_own, s, u), sub(z_own, to, u), z_send.at[way, s, u], z_recv.at[to, u], right if way == 0 else left)
        cp.start()
        z_copies.append(cp)

    def share(s):
        cp = copy(z_own.at[s], z_oth.at[s], d_send.at[s], d_recv.at[s], mate)
        cp.start()
        return cp

    shares = []

    def arrived(s, u):
        pltpu.make_async_copy(sub(z_own, s, u), sub(z_own, s, u), z_recv.at[s, u]).wait()

    for u in range(PIECES):
        ring(0, u, 0)
        ring(0, PIECES - 1 - u, 1)
    shares.append(share(0))
    for s in range(1, 4):
        if s == CROSS_AT:
            for r in range(2):
                c_copy(1, r).start()
        for u in range(PIECES):
            arrived(s, u)
            if s < 3 or u < PIECES // 2:
                ring(s, u, 0)
            w = PIECES - 1 - u
            arrived(8 - s, w)
            if s < 3 or w >= PIECES // 2:
                ring(8 - s, w, 1)
        shares.append(share(s))
        shares.append(share(8 - s))
    for v in range(PIECES // 2):
        for u in (v, PIECES - 1 - v):
            arrived(4, u)
    shares.append(share(4))
    for cp in sel_copies:
        cp.wait()
    own_sel.wait()
    pltpu.sync_copy(sel_buf, sel_sm)
    for cp in shares:
        cp.wait()

    row_is = lax.broadcasted_iota(jnp.int32, (128, 128), 0)
    col_is = lax.broadcasted_iota(jnp.int32, (128, 128), 1)

    def gram(d):
        for i in range(4):
            j = sel_sm[d, lax.rem(i + core, 4), 0]
            choice = sel_buf[d, pl.ds(lax.rem(i + core, 4), 1), :]
            last0 = 2 * x + 1
            last1 = 15 - 2 * x
            below = 2 * (x + 1) + jnp.minimum(j, last1)
            at = slice(128 * i, 128 * i + 128)
            for n, ref in enumerate((z_own, z_oth)):
                part = ref[:, :, j].reshape(128, 128)
                s_high[256 * n : 256 * n + 128, at], s_low[256 * n : 256 * n + 128, at] = split(
                    jnp.where(choice <= last0, part, 0.0)
                )
                part = ref[:, :, below].reshape(128, 128)
                s_high[256 * n + 128 : 256 * n + 256, at], s_low[256 * n + 128 : 256 * n + 256, at] = split(
                    jnp.where(choice <= last1, part, 0.0)
                )

        def cols(a, b):
            return s_high[:, a:b], s_low[:, a:b]

        first = dot(cols(0, 128), cols(0, 384), axis=0)
        second = dot(cols(256, 384), cols(256, 512), axis=0)
        a_send[d, 0:128, 0:128] = jnp.where(
            row_is > col_is, 2.0 * first[:, 0:128], jnp.where(row_is == col_is, first[:, 0:128], 2.0 * second[:, 0:128])
        )
        a_send[d, 128:136, 0:128] = jnp.broadcast_to(
            jnp.sum(jnp.where(row_is == col_is, second[:, 0:128], 0.0), axis=0, keepdims=True), (8, 128)
        )
        a_send[d, 0:128, 128:384] = 2.0 * first[:, 128:384]
        a_send[d, 0:128, 384:512] = 2.0 * second[:, 128:256]

    x_next = device(ylo, lax.rem(x + 1, 4), z, blk)
    x_last = device(ylo, lax.rem(x + 3, 4), z, blk)
    top, bottom = pl.ds(0, 64), pl.ds(64, 72)
    x_copies = [
        copy(a_send.at[2, top], a_pass.at[pl.ds(0, 64)], x_send.at[0], x_recv.at[0], x_next),
        copy(a_send.at[2, bottom], a_pass.at[pl.ds(64, 72)], x_send.at[1], x_recv.at[1], x_last),
        copy(a_send.at[1, bottom], a_recv.at[0, bottom], x_send.at[2], x_recv.at[2], x_next),
        copy(a_send.at[3, top], a_recv.at[1, top], x_send.at[3], x_recv.at[3], x_last),
        copy(a_send.at[1, top], a_recv.at[0, top], x_send.at[4], x_recv.at[4], x_next),
        copy(a_send.at[3, bottom], a_recv.at[1, bottom], x_send.at[5], x_recv.at[5], x_last),
    ]
    gram(2)
    x_copies[0].start()
    x_copies[1].start()
    for r in range(4):

        @pl.when(r >= across_blk)
        def _():
            f_copy(1, r).wait_recv()
            f_copy(2, r).start()

    gram(1)
    x_copies[2].start()
    gram(3)
    x_copies[3].start()
    gram(0)
    x_copies[0].wait_recv()
    a_send[1, 0:64, :] = a_send[1, 0:64, :] + a_pass[0:64, :]
    x_copies[4].start()
    x_copies[1].wait_recv()
    a_send[3, 64:136, :] = a_send[3, 64:136, :] + a_pass[64:136, :]
    x_copies[5].start()

    for r in range(2):
        c_copy(1, r).wait_recv()
        c_copy(2, r).start()
    for r in range(4):

        @pl.when(r >= blk)
        def _():
            f_own[r].wait()

        @pl.when(r >= mate_blk)
        def _():
            f_copy(0, r).wait_recv()

        @pl.when(r >= far_blk)
        def _():
            f_copy(2, r).wait_recv()

    square = jnp.zeros((1, 512), jnp.float32)
    for r in range(4):
        rows = slice(256 * r, 256 * r + 256)
        acc = jnp.zeros((256, 512), jnp.float32)
        for s in range(r + 1):
            at = slice(256 * s, 256 * s + 256)
            acc = acc + dot(split(f_buf[s, rows, :]), (j_high[at, :], j_low[at, :]))
        v_high[rows, :], v_low[rows, :] = split(acc)
        square = square + jnp.sum(acc * acc, axis=0, keepdims=True)

    for r in range(2):
        c_own[r].wait()
        c_copy(0, r).wait_recv()
        c_copy(2, r).wait_recv()
    for q in range(4):
        rows = lax.broadcasted_iota(jnp.int32, (128, 512), 0) + q * 128
        root = jnp.zeros((128, 512), jnp.float32)
        for k in range(2):
            root = root + jnp.where(rows == jri_ref[k : k + 1, :], jrv_ref[k : k + 1, :], 0.0)
        acc = -root
        for s in range(4):
            at = slice(256 * s, 256 * s + 256)
            acc = acc + dot(split(c_buf[s, 128 * q : 128 * q + 128, :]), (v_high[at, :], v_low[at, :]))
        at = slice(128 * q, 128 * q + 128)
        g_buf[at, :] = acc
        g_high[at, :], g_low[at, :] = split(acc)
        if q == 0:
            g_buf[512:640, :] = acc
            g_high[512:640, :], g_low[512:640, :] = split(acc)

    for cp in x_copies[2:]:
        cp.wait_recv()
    a_sum[0] = a_send[0] + a_recv[0] + a_recv[1]
    a_share = copy(a_sum.at[0], a_sum.at[1], as_send, as_recv, mate)
    a_share.start()

    def quad(n, c):
        both = a_sum[n, 0:128, 0:128]
        lower = jnp.where(row_is >= col_is, both, 0.0)
        diagonal = jnp.where(row_is == col_is, a_sum[n, 128:129, 0:128], 0.0)
        upper_ = jnp.where(row_is < col_is, both, diagonal)
        total = jnp.zeros((1, 512), jnp.float32)
        for corner, a, b, off in ((lower, 128, 384, 0), (upper_, 384, 512, 256)):
            start = pl.multiple_of(c * 128 + off, 128)
            near_ = pl.ds(start, 128)
            after = pl.ds(pl.multiple_of(start + 128, 128), b - a)
            w = dot(split(corner), (g_high[near_, :], g_low[near_, :]))
            w = w + dot(split(a_sum[n, 0:128, a:b]), (g_high[after, :], g_low[after, :]))
            total = total + jnp.sum(w * g_buf[near_, :], axis=0, keepdims=True)
        return total

    omega = noise_ref[...] + square + quad(0, core)
    a_share.wait()
    omega = omega + quad(1, 1 - core)
    live = lax.broadcasted_iota(jnp.int32, (1, 512), 1) < count_ref[0]
    out_ref[...] = jnp.where(live, resid_ref[...] / jnp.sqrt(omega), 0.0)

    for n in (1, 2):

        @pl.when(tiles_out == n)
        def _():
            for key in spread:

                @pl.when(jnp.logical_not(spread_mine(*key)))
                def _():
                    copy(*spread_copy(n, *key)).wait_send()

    for cp in z_copies:
        cp.wait_send()
    for cp in x_copies:
        cp.wait_send()
    for r in range(4):

        @pl.when(r >= blk)
        def _():
            f_copy(0, r).wait_send()
            f_copy(1, r).wait_send()

        @pl.when(r >= across_blk)
        def _():
            f_copy(2, r).wait_send()

    for r in range(2):
        for kind in range(3):
            c_copy(kind, r).wait_send()


def per_device(root, front, coupling, blocks, jci, jcv, jri, jrv, resid, noise, count):
    vmem = pl.BlockSpec(memory_space=pltpu.VMEM)
    dma = pltpu.SemaphoreType.DMA
    f32, bf16 = jnp.float32, jnp.bfloat16
    out = pl.pallas_call(
        kernel,
        out_shape=jax.ShapeDtypeStruct((1, 512), f32),
        in_specs=[pl.BlockSpec(memory_space=pltpu.HBM)] * 11,
        out_specs=vmem,
        scratch_shapes=[
            pltpu.VMEM((32, 512), f32),
            pltpu.VMEM((8, 128), jnp.int32),
            pltpu.VMEM((6, 512), jnp.int32),
            pltpu.VMEM((6, 512), f32),
            pltpu.VMEM((2, 512), jnp.int32),
            pltpu.VMEM((2, 512), f32),
            pltpu.VMEM((1, 512), f32),
            pltpu.VMEM((1, 512), f32),
            pltpu.SMEM((1, 4), jnp.int32),
            pltpu.SMEM((1,), jnp.int32),
            dma((9,)),
            pltpu.VMEM((2, 2, 4, 8, 128), f32),
            pltpu.VMEM((8, 2, TILES, 8, 128), f32),
            pltpu.VMEM((8, 2, TILES, 8, 128), f32),
            pltpu.VMEM((4, 1024, 256), f32),
            pltpu.VMEM((4, 512, 256), f32),
            pltpu.VMEM((1024, 512), bf16),
            pltpu.VMEM((1024, 512), bf16),
            pltpu.VMEM((1024, 512), bf16),
            pltpu.VMEM((1024, 512), bf16),
            pltpu.VMEM((640, 512), f32),
            pltpu.VMEM((640, 512), bf16),
            pltpu.VMEM((640, 512), bf16),
            pltpu.VMEM((512, 512), bf16),
            pltpu.VMEM((512, 512), bf16),
            pltpu.VMEM((4, 136, 512), f32),
            pltpu.VMEM((136, 512), f32),
            pltpu.VMEM((2, 136, 512), f32),
            pltpu.VMEM((2, 136, 512), f32),
            pltpu.VMEM((4, 8, 128), jnp.int32),
            pltpu.SMEM((4, 8, 128), jnp.int32),
            dma((2, 4)), dma((6,)), dma((2, 8, PIECES)), dma((8, PIECES)), dma((8,)), dma((8,)),
            dma((4,)), dma((4,)),
            dma((3, 4)), dma((4, 4)), dma((3, 2)), dma((4, 2)),
            dma((6,)), dma((6,)), dma, dma,
        ],
        compiler_params=pltpu.CompilerParams(
            collective_id=0, has_side_effects=True, vmem_limit_bytes=63 << 20
        ),
        name="selected_inverse",
    )(
        root, front, coupling, blocks, jci, jcv, jri, jrv,
        resid.reshape(1, -1), noise.reshape(1, -1), count,
    )
    return out.reshape(-1)


def solution(mesh):
    placed = (
        P("leaf", "blk"),
        P("leaf", "blk"),
        P("leaf", "blk"),
        P("leaf", None),
        P(None, ("leaf", "blk")),
        P(None, ("leaf", "blk")),
        P(None, ("leaf", "blk")),
        P(None, ("leaf", "blk")),
        P(("leaf", "blk")),
        P(("leaf", "blk")),
        P(("leaf", "blk")),
    )
    return jax.shard_map(
        per_device, mesh=mesh, in_specs=placed, out_specs=P(("leaf", "blk")), check_vma=False
    )
```

```python
import functools

import jax
import jax.numpy as jnp
from jax import lax
from jax.experimental import pallas as pl
from jax.experimental.pallas import tpu as pltpu
from jax.sharding import PartitionSpec as P

MESH = pl.DeviceIdType.MESH
CROSS_AT = 2
PIECES = 4
TILES = 18


def split(a):
    high = a.astype(jnp.bfloat16)
    return high, (a - high.astype(jnp.float32)).astype(jnp.bfloat16)


def dot(a, b, axis=1):
    def one(p, q):
        return lax.dot_general(p, q, (((axis,), (0,)), ((), ())), preferred_element_type=jnp.float32)

    return one(a[0], b[0]) + (one(a[0], b[1]) + one(a[1], b[0]))


def kernel(
    l_hbm, f_ref, c_ref, sel_hbm, jci_hbm, jcv_hbm, jri_hbm, jrv_hbm, resid_hbm, noise_hbm, count_hbm,
    out_ref,
    l_ref, sel_ref, jci_ref, jcv_ref, jri_ref, jrv_ref, resid_ref, noise_ref, sel_own, count_ref, in_sem,
    l_buf, z_own, z_oth, f_buf, c_buf, j_high, j_low, v_high, v_low, g_buf, g_high, g_low, s_high, s_low,
    a_send, a_pass, a_recv, a_sum, sel_buf, sel_sm,
    l_send, l_recv, z_send, z_recv, d_send, d_recv, sel_send, sel_recv,
    fc_send, fc_recv, cc_send, cc_recv, x_send, x_recv, as_send, as_recv,
):
    leaf = lax.axis_index("leaf")
    blk = lax.axis_index("blk")
    ylo, x, z = lax.div(leaf, 32), lax.rem(lax.div(leaf, 8), 4), lax.rem(leaf, 8)
    yhi, core = lax.div(blk, 2), lax.rem(blk, 2)

    def device(ylo_d, x_d, z_d, blk_d):
        return {"leaf": ylo_d * 32 + x_d * 8 + z_d, "blk": blk_d}

    def copy(src, dst, send, recv, to):
        return pltpu.make_async_remote_copy(
            src_ref=src, dst_ref=dst, send_sem=send, recv_sem=recv, device_id=to, device_id_type=MESH
        )

    zr, zl = lax.rem(z + 1, 8), lax.rem(z + 7, 8)
    right, left = device(ylo, x, zr, blk), device(ylo, x, zl, blk)
    mate_blk = 2 * yhi + 1 - core
    mate = device(ylo, x, z, mate_blk)
    across_blk = 2 * (1 - yhi) + core
    across = device(ylo, x, z, across_blk)
    far_blk = 2 * (1 - yhi) + 1 - core

    loads = [
        pltpu.make_async_copy(src, dst, in_sem.at[n])
        for n, (src, dst) in enumerate(
            [
                (l_hbm, l_ref), (sel_hbm, sel_own), (jci_hbm, jci_ref), (jcv_hbm, jcv_ref), (jri_hbm, jri_ref),
                (jrv_hbm, jrv_ref), (resid_hbm, resid_ref), (noise_hbm, noise_ref), (count_hbm, count_ref),
            ]
        )
    ]
    loads[0].start()
    a_send[:, 128:136, :] = jnp.zeros((4, 8, 512), jnp.float32)

    barrier = pltpu.get_barrier_semaphore()
    mirror = 3 - x
    near = lax.rem(x + jnp.where(lax.rem(x, 2) == 0, 1, 3), 4)
    partners = [right, left, device(ylo, lax.rem(x + 2, 4), z, blk), device(ylo, near, z, blk)]
    for ylo_d in range(2):
        for blk_d in range(4):
            partners.append(device(ylo_d, mirror, z, blk_d))
    for d_ylo in range(2):
        for d_blk in range(4):
            if (d_ylo, d_blk) != (0, 0):
                partners.append(device(lax.rem(ylo + d_ylo, 2), x, z, lax.rem(blk + d_blk, 4)))
    for p in partners:
        pl.semaphore_signal(barrier, inc=1, device_id=p, device_id_type=MESH)
    for cp in loads[1:]:
        cp.start()
    loads[0].wait()
    for h in range(2):
        for core_d in range(2):
            for u in range(2):
                for q in range(2):
                    r, c = 16 * core_d + 8 * u, 256 * h + 128 * q
                    l_buf[core_d, u, 2 * h + q] = l_ref[r : r + 8, c : c + 128]
    pl.semaphore_wait(barrier, len(partners))

    upper = ylo == 0
    spread = [(ylo_d, blk_d) for ylo_d in range(2) for blk_d in range(4)]
    x_to = jnp.where(upper, x, mirror)
    slot_to = jnp.where(upper, 0, 4 - x) + 2 * blk
    tiles_out = jnp.clip(jnp.where(upper, x, 4 + x) + 1 - 2 * blk, 0, 2)

    def spread_copy(n, ylo_d, blk_d):
        return (
            l_buf.at[blk_d % 2, :, pl.ds(0, 2 * n)], z_own.at[0, :, pl.ds(2 * slot_to, 2 * n)],
            l_send.at[ylo_d, blk_d], l_recv.at[jnp.where(upper, blk, 2 + blk)], device(ylo_d, x_to, z, blk_d),
        )

    def spread_mine(ylo_d, blk_d):
        return upper & (ylo_d == ylo) & (blk_d == blk)

    for n in (1, 2):

        @pl.when(tiles_out == n)
        def _():
            for key in spread:
                mine = spread_mine(*key)

                @pl.when(jnp.logical_not(mine))
                def _():
                    copy(*spread_copy(n, *key)).start()

                @pl.when(mine)
                def _():
                    src, dst, _, sem, _ = spread_copy(n, *key)
                    pltpu.make_async_copy(src, dst, sem).start()

    loads[1].wait()
    row = lax.broadcasted_iota(jnp.int32, (8, 128), 0)
    choices = jnp.zeros((8, 128), jnp.int32)
    for i in range(4):
        choices = jnp.where(row == i, sel_own[0, i], choices)
    sel_ref[...] = choices
    sel_copies = []
    for d in range(1, 4):
        cp = copy(
            sel_ref, sel_buf.at[4 - d], sel_send.at[d], sel_recv.at[4 - d],
            device(ylo, lax.rem(x + d, 4), z, blk),
        )
        cp.start()
        sel_copies.append(cp)
    own_sel = pltpu.make_async_copy(sel_ref, sel_buf.at[0], sel_recv.at[0])
    own_sel.start()

    def f_rows(r):
        return pl.ds(256 * r, 256)

    def f_copy(kind, r):
        if kind == 0:
            return copy(f_ref.at[f_rows(r)], f_buf.at[blk, f_rows(r)], fc_send.at[0, r], fc_recv.at[0, r], mate)
        if kind == 1:
            return copy(f_ref.at[f_rows(r)], f_buf.at[blk, f_rows(r)], fc_send.at[1, r], fc_recv.at[1, r], across)
        return copy(
            f_buf.at[across_blk, f_rows(r)], f_buf.at[across_blk, f_rows(r)], fc_send.at[2, r], fc_recv.at[2, r], mate
        )

    def c_copy(kind, r):
        if kind == 0:
            return copy(c_ref.at[f_rows(r)], c_buf.at[blk, f_rows(r)], cc_send.at[0, r], cc_recv.at[0, r], mate)
        if kind == 1:
            return copy(c_ref.at[f_rows(r)], c_buf.at[blk, f_rows(r)], cc_send.at[1, r], cc_recv.at[1, r], across)
        return copy(
            c_buf.at[across_blk, f_rows(r)], c_buf.at[across_blk, f_rows(r)], cc_send.at[2, r], cc_recv.at[2, r], mate
        )

    f_own = [pltpu.make_async_copy(f_ref.at[f_rows(r)], f_buf.at[blk, f_rows(r)], fc_recv.at[3, r]) for r in range(4)]
    c_own = [pltpu.make_async_copy(c_ref.at[f_rows(r)], c_buf.at[blk, f_rows(r)], cc_recv.at[3, r]) for r in range(2)]

    for kind in (1, 0):
        for r in range(4):

            @pl.when(r >= blk)
            def _():
                f_copy(kind, r).start()

    for r in range(4):

        @pl.when(r >= blk)
        def _():
            f_own[r].start()

    for r in range(2):
        c_copy(0, r).start()
        c_own[r].start()

    for cp in loads[2:]:
        cp.wait()

    @pl.loop(0, 16)
    def _(i):
        rows = lax.broadcasted_iota(jnp.int32, (64, 512), 0) + i * 64
        acc = jnp.zeros((64, 512), jnp.float32)
        for k in range(6):
            acc = acc + jnp.where(rows == jci_ref[k : k + 1, :], jcv_ref[k : k + 1, :], 0.0)
        at = pl.ds(pl.multiple_of(i * 64, 64), 64)
        j_high[at, :], j_low[at, :] = split(acc)

    for source in range(6):
        half, b = source // 2 > 0, source if source < 2 else source - 2
        tiles_in = jnp.clip((7 - x if half else x) + 1 - 2 * b, 0, 2)
        first = (x + 1 if half else 0) + 2 * b
        for n in (1, 2):

            @pl.when(tiles_in == n)
            def _():
                area = z_own.at[0, :, pl.ds(2 * first, 2 * n)]
                pltpu.make_async_copy(area, area, l_recv.at[source]).wait()

    def sub(ref, s, u):
        return ref.at[s, u // (PIECES // 2), pl.ds(u % (PIECES // 2) * (2 * TILES // PIECES), 2 * TILES // PIECES)]

    z_copies = []

    def ring(s, u, way):
        to = s + 1 if way == 0 else (s + 7) % 8
        cp = copy(sub(z_own, s, u), sub(z_own, to, u), z_send.at[way, s, u], z_recv.at[to, u], right if way == 0 else left)
        cp.start()
        z_copies.append(cp)

    def share(s):
        cp = copy(z_own.at[s], z_oth.at[s], d_send.at[s], d_recv.at[s], mate)
        cp.start()
        return cp

    shares = []

    def arrived(s, u):
        pltpu.make_async_copy(sub(z_own, s, u), sub(z_own, s, u), z_recv.at[s, u]).wait()

    for u in range(PIECES):
        ring(0, u, 0)
        ring(0, PIECES - 1 - u, 1)
    shares.append(share(0))
    for s in range(1, 4):
        if s == CROSS_AT:
            for r in range(2):
                c_copy(1, r).start()
        for u in range(PIECES):
            arrived(s, u)
            if s < 3 or u < PIECES // 2:
                ring(s, u, 0)
            w = PIECES - 1 - u
            arrived(8 - s, w)
            if s < 3 or w >= PIECES // 2:
                ring(8 - s, w, 1)
        shares.append(share(s))
        shares.append(share(8 - s))
    for v in range(PIECES // 2):
        for u in (v, PIECES - 1 - v):
            arrived(4, u)
    shares.append(share(4))
    for cp in sel_copies:
        cp.wait()
    own_sel.wait()
    pltpu.sync_copy(sel_buf, sel_sm)
    for cp in shares:
        cp.wait()

    row_is = lax.broadcasted_iota(jnp.int32, (128, 128), 0)
    col_is = lax.broadcasted_iota(jnp.int32, (128, 128), 1)

    def gram(d):
        for i in range(4):
            j = sel_sm[d, lax.rem(i + core, 4), 0]
            choice = sel_buf[d, pl.ds(lax.rem(i + core, 4), 1), :]
            last0 = 2 * x + 1
            last1 = 15 - 2 * x
            below = 2 * (x + 1) + jnp.minimum(j, last1)
            at = slice(128 * i, 128 * i + 128)
            for n, ref in enumerate((z_own, z_oth)):
                part = ref[:, :, j].reshape(128, 128)
                s_high[256 * n : 256 * n + 128, at], s_low[256 * n : 256 * n + 128, at] = split(
                    jnp.where(choice <= last0, part, 0.0)
                )
                part = ref[:, :, below].reshape(128, 128)
                s_high[256 * n + 128 : 256 * n + 256, at], s_low[256 * n + 128 : 256 * n + 256, at] = split(
                    jnp.where(choice <= last1, part, 0.0)
                )

        def cols(a, b):
            return s_high[:, a:b], s_low[:, a:b]

        first = dot(cols(0, 128), cols(0, 384), axis=0)
        second = dot(cols(256, 384), cols(256, 512), axis=0)
        a_send[d, 0:128, 0:128] = jnp.where(
            row_is > col_is, 2.0 * first[:, 0:128], jnp.where(row_is == col_is, first[:, 0:128], 2.0 * second[:, 0:128])
        )
        a_send[d, 128:136, 0:128] = jnp.broadcast_to(
            jnp.sum(jnp.where(row_is == col_is, second[:, 0:128], 0.0), axis=0, keepdims=True), (8, 128)
        )
        a_send[d, 0:128, 128:384] = 2.0 * first[:, 128:384]
        a_send[d, 0:128, 384:512] = 2.0 * second[:, 128:256]

    x_next = device(ylo, lax.rem(x + 1, 4), z, blk)
    x_last = device(ylo, lax.rem(x + 3, 4), z, blk)
    top, bottom = pl.ds(0, 64), pl.ds(64, 72)
    x_copies = [
        copy(a_send.at[2, top], a_pass.at[pl.ds(0, 64)], x_send.at[0], x_recv.at[0], x_next),
        copy(a_send.at[2, bottom], a_pass.at[pl.ds(64, 72)], x_send.at[1], x_recv.at[1], x_last),
        copy(a_send.at[1, bottom], a_recv.at[0, bottom], x_send.at[2], x_recv.at[2], x_next),
        copy(a_send.at[3, top], a_recv.at[1, top], x_send.at[3], x_recv.at[3], x_last),
        copy(a_send.at[1, top], a_recv.at[0, top], x_send.at[4], x_recv.at[4], x_next),
        copy(a_send.at[3, bottom], a_recv.at[1, bottom], x_send.at[5], x_recv.at[5], x_last),
    ]
    gram(2)
    x_copies[0].start()
    x_copies[1].start()
    for r in range(4):

        @pl.when(r >= across_blk)
        def _():
            f_copy(1, r).wait_recv()
            f_copy(2, r).start()

    gram(1)
    x_copies[2].start()
    gram(3)
    x_copies[3].start()
    gram(0)
    x_copies[0].wait_recv()
    a_send[1, 0:64, :] = a_send[1, 0:64, :] + a_pass[0:64, :]
    x_copies[4].start()
    x_copies[1].wait_recv()
    a_send[3, 64:136, :] = a_send[3, 64:136, :] + a_pass[64:136, :]
    x_copies[5].start()

    for r in range(4):

        @pl.when(r >= blk)
        def _():
            f_own[r].wait()

        @pl.when(r >= mate_blk)
        def _():
            f_copy(0, r).wait_recv()

        @pl.when(r >= far_blk)
        def _():
            f_copy(2, r).wait_recv()

    square = jnp.zeros((1, 512), jnp.float32)
    for r in range(4):
        rows = slice(256 * r, 256 * r + 256)
        acc = jnp.zeros((256, 512), jnp.float32)
        for s in range(r + 1):
            at = slice(256 * s, 256 * s + 256)
            acc = acc + dot(split(f_buf[s, rows, :]), (j_high[at, :], j_low[at, :]))
        v_high[rows, :], v_low[rows, :] = split(acc)
        square = square + jnp.sum(acc * acc, axis=0, keepdims=True)
        if r == 2:
            for r in range(2):
                c_copy(1, r).wait_recv()
                c_copy(2, r).start()

    for q in range(4):
        if q % 2 == 0:
            c_own[q // 2].wait()
            c_copy(0, q // 2).wait_recv()
            c_copy(2, q // 2).wait_recv()
        rows = lax.broadcasted_iota(jnp.int32, (128, 512), 0) + q * 128
        root = jnp.zeros((128, 512), jnp.float32)
        for k in range(2):
            root = root + jnp.where(rows == jri_ref[k : k + 1, :], jrv_ref[k : k + 1, :], 0.0)
        acc = -root
        for s in range(4):
            at = slice(256 * s, 256 * s + 256)
            acc = acc + dot(split(c_buf[s, 128 * q : 128 * q + 128, :]), (v_high[at, :], v_low[at, :]))
        at = slice(128 * q, 128 * q + 128)
        g_buf[at, :] = acc
        g_high[at, :], g_low[at, :] = split(acc)
        if q == 0:
            g_buf[512:640, :] = acc
            g_high[512:640, :], g_low[512:640, :] = split(acc)

    for cp in x_copies[2:]:
        cp.wait_recv()
    a_sum[0] = a_send[0] + a_recv[0] + a_recv[1]
    a_share = copy(a_sum.at[0], a_sum.at[1], as_send, as_recv, mate)
    a_share.start()

    def quad(n, c):
        both = a_sum[n, 0:128, 0:128]
        lower = jnp.where(row_is >= col_is, both, 0.0)
        diagonal = jnp.where(row_is == col_is, a_sum[n, 128:129, 0:128], 0.0)
        upper_ = jnp.where(row_is < col_is, both, diagonal)
        total = jnp.zeros((1, 512), jnp.float32)
        for corner, a, b, off in ((lower, 128, 384, 0), (upper_, 384, 512, 256)):
            start = pl.multiple_of(c * 128 + off, 128)
            near_ = pl.ds(start, 128)
            after = pl.ds(pl.multiple_of(start + 128, 128), b - a)
            w = dot(split(corner), (g_high[near_, :], g_low[near_, :]))
            w = w + dot(split(a_sum[n, 0:128, a:b]), (g_high[after, :], g_low[after, :]))
            total = total + jnp.sum(w * g_buf[near_, :], axis=0, keepdims=True)
        return total

    omega = noise_ref[...] + square + quad(0, core)
    a_share.wait()
    omega = omega + quad(1, 1 - core)
    live = lax.broadcasted_iota(jnp.int32, (1, 512), 1) < count_ref[0]
    out_ref[...] = jnp.where(live, resid_ref[...] / jnp.sqrt(omega), 0.0)

    for n in (1, 2):

        @pl.when(tiles_out == n)
        def _():
            for key in spread:

                @pl.when(jnp.logical_not(spread_mine(*key)))
                def _():
                    copy(*spread_copy(n, *key)).wait_send()

    for cp in z_copies:
        cp.wait_send()
    for cp in x_copies:
        cp.wait_send()
    for r in range(4):

        @pl.when(r >= blk)
        def _():
            f_copy(0, r).wait_send()
            f_copy(1, r).wait_send()

        @pl.when(r >= across_blk)
        def _():
            f_copy(2, r).wait_send()

    for r in range(2):
        for kind in range(3):
            c_copy(kind, r).wait_send()


def per_device(root, front, coupling, blocks, jci, jcv, jri, jrv, resid, noise, count):
    vmem = pl.BlockSpec(memory_space=pltpu.VMEM)
    dma = pltpu.SemaphoreType.DMA
    f32, bf16 = jnp.float32, jnp.bfloat16
    out = pl.pallas_call(
        kernel,
        out_shape=jax.ShapeDtypeStruct((1, 512), f32),
        in_specs=[pl.BlockSpec(memory_space=pltpu.HBM)] * 11,
        out_specs=vmem,
        scratch_shapes=[
            pltpu.VMEM((32, 512), f32),
            pltpu.VMEM((8, 128), jnp.int32),
            pltpu.VMEM((6, 512), jnp.int32),
            pltpu.VMEM((6, 512), f32),
            pltpu.VMEM((2, 512), jnp.int32),
            pltpu.VMEM((2, 512), f32),
            pltpu.VMEM((1, 512), f32),
            pltpu.VMEM((1, 512), f32),
            pltpu.SMEM((1, 4), jnp.int32),
            pltpu.SMEM((1,), jnp.int32),
            dma((9,)),
            pltpu.VMEM((2, 2, 4, 8, 128), f32),
            pltpu.VMEM((8, 2, TILES, 8, 128), f32),
            pltpu.VMEM((8, 2, TILES, 8, 128), f32),
            pltpu.VMEM((4, 1024, 256), f32),
            pltpu.VMEM((4, 512, 256), f32),
            pltpu.VMEM((1024, 512), bf16),
            pltpu.VMEM((1024, 512), bf16),
            pltpu.VMEM((1024, 512), bf16),
            pltpu.VMEM((1024, 512), bf16),
            pltpu.VMEM((640, 512), f32),
            pltpu.VMEM((640, 512), bf16),
            pltpu.VMEM((640, 512), bf16),
            pltpu.VMEM((512, 512), bf16),
            pltpu.VMEM((512, 512), bf16),
            pltpu.VMEM((4, 136, 512), f32),
            pltpu.VMEM((136, 512), f32),
            pltpu.VMEM((2, 136, 512), f32),
            pltpu.VMEM((2, 136, 512), f32),
            pltpu.VMEM((4, 8, 128), jnp.int32),
            pltpu.SMEM((4, 8, 128), jnp.int32),
            dma((2, 4)), dma((6,)), dma((2, 8, PIECES)), dma((8, PIECES)), dma((8,)), dma((8,)),
            dma((4,)), dma((4,)),
            dma((3, 4)), dma((4, 4)), dma((3, 2)), dma((4, 2)),
            dma((6,)), dma((6,)), dma, dma,
        ],
        compiler_params=pltpu.CompilerParams(
            collective_id=0, has_side_effects=True, vmem_limit_bytes=63 << 20
        ),
        name="selected_inverse",
    )(
        root, front, coupling, blocks, jci, jcv, jri, jrv,
        resid.reshape(1, -1), noise.reshape(1, -1), count,
    )
    return out.reshape(-1)


def solution(mesh):
    placed = (
        P("leaf", "blk"),
        P("leaf", "blk"),
        P("leaf", "blk"),
        P("leaf", None),
        P(None, ("leaf", "blk")),
        P(None, ("leaf", "blk")),
        P(None, ("leaf", "blk")),
        P(None, ("leaf", "blk")),
        P(("leaf", "blk")),
        P(("leaf", "blk")),
        P(("leaf", "blk")),
    )
    return jax.shard_map(
        per_device, mesh=mesh, in_specs=placed, out_specs=P(("leaf", "blk")), check_vma=False
    )
```

```python
import functools

import jax
import jax.numpy as jnp
from jax import lax
from jax.experimental import pallas as pl
from jax.experimental.pallas import tpu as pltpu
from jax.sharding import PartitionSpec as P

MESH = pl.DeviceIdType.MESH
CROSS_AT = 2
PIECES = 4
TILES = 18


def split(a):
    high = a.astype(jnp.bfloat16)
    return high, (a - high.astype(jnp.float32)).astype(jnp.bfloat16)


def dot(a, b, axis=1):
    def one(p, q):
        return lax.dot_general(p, q, (((axis,), (0,)), ((), ())), preferred_element_type=jnp.float32)

    return one(a[0], b[0]) + (one(a[0], b[1]) + one(a[1], b[0]))


def kernel(
    l_hbm, f_ref, c_ref, sel_hbm, jci_hbm, jcv_hbm, jri_hbm, jrv_hbm, resid_hbm, noise_hbm, count_hbm,
    out_ref,
    l_ref, sel_ref, jci_ref, jcv_ref, jri_ref, jrv_ref, resid_ref, noise_ref, sel_own, count_ref, in_sem,
    l_buf, z_own, z_oth, f_buf, c_buf, j_high, j_low, v_high, v_low, g_buf, g_high, g_low, s_high, s_low,
    a_send, a_pass, a_recv, a_sum, sel_buf, sel_sm,
    l_send, l_recv, z_send, z_recv, d_send, d_recv, sel_send, sel_recv,
    fc_send, fc_recv, cc_send, cc_recv, x_send, x_recv, as_send, as_recv,
):
    leaf = lax.axis_index("leaf")
    blk = lax.axis_index("blk")
    ylo, x, z = lax.div(leaf, 32), lax.rem(lax.div(leaf, 8), 4), lax.rem(leaf, 8)
    yhi, core = lax.div(blk, 2), lax.rem(blk, 2)

    def device(ylo_d, x_d, z_d, blk_d):
        return {"leaf": ylo_d * 32 + x_d * 8 + z_d, "blk": blk_d}

    def copy(src, dst, send, recv, to):
        return pltpu.make_async_remote_copy(
            src_ref=src, dst_ref=dst, send_sem=send, recv_sem=recv, device_id=to, device_id_type=MESH
        )

    zr, zl = lax.rem(z + 1, 8), lax.rem(z + 7, 8)
    right, left = device(ylo, x, zr, blk), device(ylo, x, zl, blk)
    mate_blk = 2 * yhi + 1 - core
    mate = device(ylo, x, z, mate_blk)
    across_blk = 2 * (1 - yhi) + core
    across = device(ylo, x, z, across_blk)
    far_blk = 2 * (1 - yhi) + 1 - core

    loads = [
        pltpu.make_async_copy(src, dst, in_sem.at[n])
        for n, (src, dst) in enumerate(
            [
                (l_hbm, l_ref), (sel_hbm, sel_own), (jci_hbm, jci_ref), (jcv_hbm, jcv_ref), (jri_hbm, jri_ref),
                (jrv_hbm, jrv_ref), (resid_hbm, resid_ref), (noise_hbm, noise_ref), (count_hbm, count_ref),
            ]
        )
    ]
    loads[0].start()
    a_send[:, 128:136, :] = jnp.zeros((4, 8, 512), jnp.float32)

    barrier = pltpu.get_barrier_semaphore()
    mirror = 3 - x
    near = lax.rem(x + jnp.where(lax.rem(x, 2) == 0, 1, 3), 4)
    partners = [right, left, device(ylo, lax.rem(x + 2, 4), z, blk), device(ylo, near, z, blk)]
    for ylo_d in range(2):
        for blk_d in range(4):
            partners.append(device(ylo_d, mirror, z, blk_d))
    for d_ylo in range(2):
        for d_blk in range(4):
            if (d_ylo, d_blk) != (0, 0):
                partners.append(device(lax.rem(ylo + d_ylo, 2), x, z, lax.rem(blk + d_blk, 4)))
    for p in partners:
        pl.semaphore_signal(barrier, inc=1, device_id=p, device_id_type=MESH)
    for cp in loads[1:]:
        cp.start()
    loads[0].wait()
    for h in range(2):
        for core_d in range(2):
            for u in range(2):
                for q in range(2):
                    r, c = 16 * core_d + 8 * u, 256 * h + 128 * q
                    l_buf[core_d, u, 2 * h + q] = l_ref[r : r + 8, c : c + 128]
    pl.semaphore_wait(barrier, len(partners))

    upper = ylo == 0
    spread = [(ylo_d, blk_d) for blk_d in range(4) for ylo_d in range(2)]
    x_to = jnp.where(upper, x, mirror)
    slot_to = jnp.where(upper, 0, 4 - x) + 2 * blk
    tiles_out = jnp.clip(jnp.where(upper, x, 4 + x) + 1 - 2 * blk, 0, 2)

    def spread_copy(n, ylo_d, blk_d):
        return (
            l_buf.at[blk_d % 2, :, pl.ds(0, 2 * n)], z_own.at[0, :, pl.ds(2 * slot_to, 2 * n)],
            l_send.at[ylo_d, blk_d], l_recv.at[jnp.where(upper, blk, 2 + blk)], device(ylo_d, x_to, z, blk_d),
        )

    def spread_mine(ylo_d, blk_d):
        return upper & (ylo_d == ylo) & (blk_d == blk)

    for n in (1, 2):

        @pl.when(tiles_out == n)
        def _():
            for key in spread:
                mine = spread_mine(*key)

                @pl.when(jnp.logical_not(mine))
                def _():
                    copy(*spread_copy(n, *key)).start()

                @pl.when(mine)
                def _():
                    src, dst, _, sem, _ = spread_copy(n, *key)
                    pltpu.make_async_copy(src, dst, sem).start()

    loads[1].wait()
    row = lax.broadcasted_iota(jnp.int32, (8, 128), 0)
    choices = jnp.zeros((8, 128), jnp.int32)
    for i in range(4):
        choices = jnp.where(row == i, sel_own[0, i], choices)
    sel_ref[...] = choices
    sel_copies = []
    for d in range(1, 4):
        cp = copy(
            sel_ref, sel_buf.at[4 - d], sel_send.at[d], sel_recv.at[4 - d],
            device(ylo, lax.rem(x + d, 4), z, blk),
        )
        cp.start()
        sel_copies.append(cp)
    own_sel = pltpu.make_async_copy(sel_ref, sel_buf.at[0], sel_recv.at[0])
    own_sel.start()

    def f_rows(r):
        return pl.ds(256 * r, 256)

    def f_copy(kind, r):
        if kind == 0:
            return copy(f_ref.at[f_rows(r)], f_buf.at[blk, f_rows(r)], fc_send.at[0, r], fc_recv.at[0, r], mate)
        if kind == 1:
            return copy(f_ref.at[f_rows(r)], f_buf.at[blk, f_rows(r)], fc_send.at[1, r], fc_recv.at[1, r], across)
        return copy(
            f_buf.at[across_blk, f_rows(r)], f_buf.at[across_blk, f_rows(r)], fc_send.at[2, r], fc_recv.at[2, r], mate
        )

    def c_copy(kind, r):
        if kind == 0:
            return copy(c_ref.at[f_rows(r)], c_buf.at[blk, f_rows(r)], cc_send.at[0, r], cc_recv.at[0, r], mate)
        if kind == 1:
            return copy(c_ref.at[f_rows(r)], c_buf.at[blk, f_rows(r)], cc_send.at[1, r], cc_recv.at[1, r], across)
        return copy(
            c_buf.at[across_blk, f_rows(r)], c_buf.at[across_blk, f_rows(r)], cc_send.at[2, r], cc_recv.at[2, r], mate
        )

    f_own = [pltpu.make_async_copy(f_ref.at[f_rows(r)], f_buf.at[blk, f_rows(r)], fc_recv.at[3, r]) for r in range(4)]
    c_own = [pltpu.make_async_copy(c_ref.at[f_rows(r)], c_buf.at[blk, f_rows(r)], cc_recv.at[3, r]) for r in range(2)]

    for kind in (1, 0):
        for r in range(4):

            @pl.when(r >= blk)
            def _():
                f_copy(kind, r).start()

    for r in range(4):

        @pl.when(r >= blk)
        def _():
            f_own[r].start()

    for r in range(2):
        c_copy(0, r).start()
        c_own[r].start()

    for cp in loads[2:]:
        cp.wait()

    @pl.loop(0, 16)
    def _(i):
        rows = lax.broadcasted_iota(jnp.int32, (64, 512), 0) + i * 64
        acc = jnp.zeros((64, 512), jnp.float32)
        for k in range(6):
            acc = acc + jnp.where(rows == jci_ref[k : k + 1, :], jcv_ref[k : k + 1, :], 0.0)
        at = pl.ds(pl.multiple_of(i * 64, 64), 64)
        j_high[at, :], j_low[at, :] = split(acc)

    for source in range(6):
        half, b = source // 2 > 0, source if source < 2 else source - 2
        tiles_in = jnp.clip((7 - x if half else x) + 1 - 2 * b, 0, 2)
        first = (x + 1 if half else 0) + 2 * b
        for n in (1, 2):

            @pl.when(tiles_in == n)
            def _():
                area = z_own.at[0, :, pl.ds(2 * first, 2 * n)]
                pltpu.make_async_copy(area, area, l_recv.at[source]).wait()

    def sub(ref, s, u):
        return ref.at[s, u // (PIECES // 2), pl.ds(u % (PIECES // 2) * (2 * TILES // PIECES), 2 * TILES // PIECES)]

    z_copies = []

    def ring(s, u, way):
        to = s + 1 if way == 0 else (s + 7) % 8
        cp = copy(sub(z_own, s, u), sub(z_own, to, u), z_send.at[way, s, u], z_recv.at[to, u], right if way == 0 else left)
        cp.start()
        z_copies.append(cp)

    def share(s):
        cp = copy(z_own.at[s], z_oth.at[s], d_send.at[s], d_recv.at[s], mate)
        cp.start()
        return cp

    shares = []

    def arrived(s, u):
        pltpu.make_async_copy(sub(z_own, s, u), sub(z_own, s, u), z_recv.at[s, u]).wait()

    for u in range(PIECES):
        ring(0, u, 0)
        ring(0, PIECES - 1 - u, 1)
    shares.append(share(0))
    for s in range(1, 4):
        if s == CROSS_AT:
            for r in range(2):
                c_copy(1, r).start()
        for u in range(PIECES):
            arrived(s, u)
            if s < 3 or u < PIECES // 2:
                ring(s, u, 0)
            w = PIECES - 1 - u
            arrived(8 - s, w)
            if s < 3 or w >= PIECES // 2:
                ring(8 - s, w, 1)
        shares.append(share(s))
        shares.append(share(8 - s))
    for v in range(PIECES // 2):
        for u in (v, PIECES - 1 - v):
            arrived(4, u)
    shares.append(share(4))
    for cp in sel_copies:
        cp.wait()
    own_sel.wait()
    pltpu.sync_copy(sel_buf, sel_sm)
    for cp in shares:
        cp.wait()

    row_is = lax.broadcasted_iota(jnp.int32, (128, 128), 0)
    col_is = lax.broadcasted_iota(jnp.int32, (128, 128), 1)

    def gram(d):
        for i in range(4):
            j = sel_sm[d, lax.rem(i + core, 4), 0]
            choice = sel_buf[d, pl.ds(lax.rem(i + core, 4), 1), :]
            last0 = 2 * x + 1
            last1 = 15 - 2 * x
            below = 2 * (x + 1) + jnp.minimum(j, last1)
            at = slice(128 * i, 128 * i + 128)
            for n, ref in enumerate((z_own, z_oth)):
                part = ref[:, :, j].reshape(128, 128)
                s_high[256 * n : 256 * n + 128, at], s_low[256 * n : 256 * n + 128, at] = split(
                    jnp.where(choice <= last0, part, 0.0)
                )
                part = ref[:, :, below].reshape(128, 128)
                s_high[256 * n + 128 : 256 * n + 256, at], s_low[256 * n + 128 : 256 * n + 256, at] = split(
                    jnp.where(choice <= last1, part, 0.0)
                )

        def cols(a, b):
            return s_high[:, a:b], s_low[:, a:b]

        first = dot(cols(0, 128), cols(0, 384), axis=0)
        second = dot(cols(256, 384), cols(256, 512), axis=0)
        a_send[d, 0:128, 0:128] = jnp.where(
            row_is > col_is, 2.0 * first[:, 0:128], jnp.where(row_is == col_is, first[:, 0:128], 2.0 * second[:, 0:128])
        )
        a_send[d, 128:136, 0:128] = jnp.broadcast_to(
            jnp.sum(jnp.where(row_is == col_is, second[:, 0:128], 0.0), axis=0, keepdims=True), (8, 128)
        )
        a_send[d, 0:128, 128:384] = 2.0 * first[:, 128:384]
        a_send[d, 0:128, 384:512] = 2.0 * second[:, 128:256]

    x_next = device(ylo, lax.rem(x + 1, 4), z, blk)
    x_last = device(ylo, lax.rem(x + 3, 4), z, blk)
    top, bottom = pl.ds(0, 64), pl.ds(64, 72)
    x_copies = [
        copy(a_send.at[2, top], a_pass.at[pl.ds(0, 64)], x_send.at[0], x_recv.at[0], x_next),
        copy(a_send.at[2, bottom], a_pass.at[pl.ds(64, 72)], x_send.at[1], x_recv.at[1], x_last),
        copy(a_send.at[1, bottom], a_recv.at[0, bottom], x_send.at[2], x_recv.at[2], x_next),
        copy(a_send.at[3, top], a_recv.at[1, top], x_send.at[3], x_recv.at[3], x_last),
        copy(a_send.at[1, top], a_recv.at[0, top], x_send.at[4], x_recv.at[4], x_next),
        copy(a_send.at[3, bottom], a_recv.at[1, bottom], x_send.at[5], x_recv.at[5], x_last),
    ]
    gram(2)
    x_copies[0].start()
    x_copies[1].start()
    for r in range(4):

        @pl.when(r >= across_blk)
        def _():
            f_copy(1, r).wait_recv()
            f_copy(2, r).start()

    gram(1)
    x_copies[2].start()
    gram(3)
    x_copies[3].start()
    gram(0)
    x_copies[0].wait_recv()
    a_send[1, 0:64, :] = a_send[1, 0:64, :] + a_pass[0:64, :]
    x_copies[4].start()
    x_copies[1].wait_recv()
    a_send[3, 64:136, :] = a_send[3, 64:136, :] + a_pass[64:136, :]
    x_copies[5].start()

    for r in range(4):

        @pl.when(r >= blk)
        def _():
            f_own[r].wait()

        @pl.when(r >= mate_blk)
        def _():
            f_copy(0, r).wait_recv()

        @pl.when(r >= far_blk)
        def _():
            f_copy(2, r).wait_recv()

    square = jnp.zeros((1, 512), jnp.float32)
    for r in range(4):
        rows = slice(256 * r, 256 * r + 256)
        acc = jnp.zeros((256, 512), jnp.float32)
        for s in range(r + 1):
            at = slice(256 * s, 256 * s + 256)
            acc = acc + dot(split(f_buf[s, rows, :]), (j_high[at, :], j_low[at, :]))
        v_high[rows, :], v_low[rows, :] = split(acc)
        square = square + jnp.sum(acc * acc, axis=0, keepdims=True)
        if r == 2:
            for r in range(2):
                c_copy(1, r).wait_recv()
                c_copy(2, r).start()

    for q in range(4):
        if q % 2 == 0:
            c_own[q // 2].wait()
            c_copy(0, q // 2).wait_recv()
            c_copy(2, q // 2).wait_recv()
        rows = lax.broadcasted_iota(jnp.int32, (128, 512), 0) + q * 128
        root = jnp.zeros((128, 512), jnp.float32)
        for k in range(2):
            root = root + jnp.where(rows == jri_ref[k : k + 1, :], jrv_ref[k : k + 1, :], 0.0)
        acc = -root
        for s in range(4):
            at = slice(256 * s, 256 * s + 256)
            acc = acc + dot(split(c_buf[s, 128 * q : 128 * q + 128, :]), (v_high[at, :], v_low[at, :]))
        at = slice(128 * q, 128 * q + 128)
        g_buf[at, :] = acc
        g_high[at, :], g_low[at, :] = split(acc)
        if q == 0:
            g_buf[512:640, :] = acc
            g_high[512:640, :], g_low[512:640, :] = split(acc)

    for cp in x_copies[2:]:
        cp.wait_recv()
    a_sum[0] = a_send[0] + a_recv[0] + a_recv[1]
    a_share = copy(a_sum.at[0], a_sum.at[1], as_send, as_recv, mate)
    a_share.start()

    def quad(n, c):
        both = a_sum[n, 0:128, 0:128]
        lower = jnp.where(row_is >= col_is, both, 0.0)
        diagonal = jnp.where(row_is == col_is, a_sum[n, 128:129, 0:128], 0.0)
        upper_ = jnp.where(row_is < col_is, both, diagonal)
        total = jnp.zeros((1, 512), jnp.float32)
        for corner, a, b, off in ((lower, 128, 384, 0), (upper_, 384, 512, 256)):
            start = pl.multiple_of(c * 128 + off, 128)
            near_ = pl.ds(start, 128)
            after = pl.ds(pl.multiple_of(start + 128, 128), b - a)
            w = dot(split(corner), (g_high[near_, :], g_low[near_, :]))
            w = w + dot(split(a_sum[n, 0:128, a:b]), (g_high[after, :], g_low[after, :]))
            total = total + jnp.sum(w * g_buf[near_, :], axis=0, keepdims=True)
        return total

    omega = noise_ref[...] + square + quad(0, core)
    a_share.wait()
    omega = omega + quad(1, 1 - core)
    live = lax.broadcasted_iota(jnp.int32, (1, 512), 1) < count_ref[0]
    out_ref[...] = jnp.where(live, resid_ref[...] / jnp.sqrt(omega), 0.0)

    for n in (1, 2):

        @pl.when(tiles_out == n)
        def _():
            for key in spread:

                @pl.when(jnp.logical_not(spread_mine(*key)))
                def _():
                    copy(*spread_copy(n, *key)).wait_send()

    for cp in z_copies:
        cp.wait_send()
    for cp in x_copies:
        cp.wait_send()
    for r in range(4):

        @pl.when(r >= blk)
        def _():
            f_copy(0, r).wait_send()
            f_copy(1, r).wait_send()

        @pl.when(r >= across_blk)
        def _():
            f_copy(2, r).wait_send()

    for r in range(2):
        for kind in range(3):
            c_copy(kind, r).wait_send()


def per_device(root, front, coupling, blocks, jci, jcv, jri, jrv, resid, noise, count):
    vmem = pl.BlockSpec(memory_space=pltpu.VMEM)
    dma = pltpu.SemaphoreType.DMA
    f32, bf16 = jnp.float32, jnp.bfloat16
    out = pl.pallas_call(
        kernel,
        out_shape=jax.ShapeDtypeStruct((1, 512), f32),
        in_specs=[pl.BlockSpec(memory_space=pltpu.HBM)] * 11,
        out_specs=vmem,
        scratch_shapes=[
            pltpu.VMEM((32, 512), f32),
            pltpu.VMEM((8, 128), jnp.int32),
            pltpu.VMEM((6, 512), jnp.int32),
            pltpu.VMEM((6, 512), f32),
            pltpu.VMEM((2, 512), jnp.int32),
            pltpu.VMEM((2, 512), f32),
            pltpu.VMEM((1, 512), f32),
            pltpu.VMEM((1, 512), f32),
            pltpu.SMEM((1, 4), jnp.int32),
            pltpu.SMEM((1,), jnp.int32),
            dma((9,)),
            pltpu.VMEM((2, 2, 4, 8, 128), f32),
            pltpu.VMEM((8, 2, TILES, 8, 128), f32),
            pltpu.VMEM((8, 2, TILES, 8, 128), f32),
            pltpu.VMEM((4, 1024, 256), f32),
            pltpu.VMEM((4, 512, 256), f32),
            pltpu.VMEM((1024, 512), bf16),
            pltpu.VMEM((1024, 512), bf16),
            pltpu.VMEM((1024, 512), bf16),
            pltpu.VMEM((1024, 512), bf16),
            pltpu.VMEM((640, 512), f32),
            pltpu.VMEM((640, 512), bf16),
            pltpu.VMEM((640, 512), bf16),
            pltpu.VMEM((512, 512), bf16),
            pltpu.VMEM((512, 512), bf16),
            pltpu.VMEM((4, 136, 512), f32),
            pltpu.VMEM((136, 512), f32),
            pltpu.VMEM((2, 136, 512), f32),
            pltpu.VMEM((2, 136, 512), f32),
            pltpu.VMEM((4, 8, 128), jnp.int32),
            pltpu.SMEM((4, 8, 128), jnp.int32),
            dma((2, 4)), dma((6,)), dma((2, 8, PIECES)), dma((8, PIECES)), dma((8,)), dma((8,)),
            dma((4,)), dma((4,)),
            dma((3, 4)), dma((4, 4)), dma((3, 2)), dma((4, 2)),
            dma((6,)), dma((6,)), dma, dma,
        ],
        compiler_params=pltpu.CompilerParams(
            collective_id=0, has_side_effects=True, vmem_limit_bytes=63 << 20
        ),
        name="selected_inverse",
    )(
        root, front, coupling, blocks, jci, jcv, jri, jrv,
        resid.reshape(1, -1), noise.reshape(1, -1), count,
    )
    return out.reshape(-1)


def solution(mesh):
    placed = (
        P("leaf", "blk"),
        P("leaf", "blk"),
        P("leaf", "blk"),
        P("leaf", None),
        P(None, ("leaf", "blk")),
        P(None, ("leaf", "blk")),
        P(None, ("leaf", "blk")),
        P(None, ("leaf", "blk")),
        P(("leaf", "blk")),
        P(("leaf", "blk")),
        P(("leaf", "blk")),
    )
    return jax.shard_map(
        per_device, mesh=mesh, in_specs=placed, out_specs=P(("leaf", "blk")), check_vma=False
    )
```

```python
import functools

import jax
import jax.numpy as jnp
from jax import lax
from jax.experimental import pallas as pl
from jax.experimental.pallas import tpu as pltpu
from jax.sharding import PartitionSpec as P

MESH = pl.DeviceIdType.MESH
CROSS_AT = 2
PIECES = 4
TILES = 18


def split(a):
    high = a.astype(jnp.bfloat16)
    return high, (a - high.astype(jnp.float32)).astype(jnp.bfloat16)


def dot(a, b, axis=1):
    def one(p, q):
        return lax.dot_general(p, q, (((axis,), (0,)), ((), ())), preferred_element_type=jnp.float32)

    return one(a[0], b[0]) + (one(a[0], b[1]) + one(a[1], b[0]))


def kernel(
    l_hbm, f_ref, c_ref, sel_hbm, jci_hbm, jcv_hbm, jri_hbm, jrv_hbm, resid_hbm, noise_hbm, count_hbm,
    out_ref,
    l_ref, sel_ref, jci_ref, jcv_ref, jri_ref, jrv_ref, resid_ref, noise_ref, sel_own, count_ref, in_sem,
    l_buf, z_own, z_oth, f_buf, c_buf, j_high, j_low, v_high, v_low, g_buf, g_high, g_low, s_high, s_low,
    a_send, a_pass, a_recv, a_sum, sel_buf, sel_sm,
    l_send, l_recv, z_send, z_recv, d_send, d_recv, sel_send, sel_recv,
    fc_send, fc_recv, cc_send, cc_recv, x_send, x_recv, as_send, as_recv,
):
    leaf = lax.axis_index("leaf")
    blk = lax.axis_index("blk")
    ylo, x, z = lax.div(leaf, 32), lax.rem(lax.div(leaf, 8), 4), lax.rem(leaf, 8)
    yhi, core = lax.div(blk, 2), lax.rem(blk, 2)

    def device(ylo_d, x_d, z_d, blk_d):
        return {"leaf": ylo_d * 32 + x_d * 8 + z_d, "blk": blk_d}

    def copy(src, dst, send, recv, to):
        return pltpu.make_async_remote_copy(
            src_ref=src, dst_ref=dst, send_sem=send, recv_sem=recv, device_id=to, device_id_type=MESH
        )

    zr, zl = lax.rem(z + 1, 8), lax.rem(z + 7, 8)
    right, left = device(ylo, x, zr, blk), device(ylo, x, zl, blk)
    mate_blk = 2 * yhi + 1 - core
    mate = device(ylo, x, z, mate_blk)
    across_blk = 2 * (1 - yhi) + core
    across = device(ylo, x, z, across_blk)
    far_blk = 2 * (1 - yhi) + 1 - core

    loads = [
        pltpu.make_async_copy(src, dst, in_sem.at[n])
        for n, (src, dst) in enumerate(
            [
                (l_hbm, l_ref), (sel_hbm, sel_own), (jci_hbm, jci_ref), (jcv_hbm, jcv_ref), (jri_hbm, jri_ref),
                (jrv_hbm, jrv_ref), (resid_hbm, resid_ref), (noise_hbm, noise_ref), (count_hbm, count_ref),
            ]
        )
    ]
    loads[0].start()
    a_send[:, 128:136, :] = jnp.zeros((4, 8, 512), jnp.float32)

    barrier = pltpu.get_barrier_semaphore()
    mirror = 3 - x
    near = lax.rem(x + jnp.where(lax.rem(x, 2) == 0, 1, 3), 4)
    partners = [right, left, device(ylo, lax.rem(x + 2, 4), z, blk), device(ylo, near, z, blk)]
    for ylo_d in range(2):
        for blk_d in range(4):
            partners.append(device(ylo_d, mirror, z, blk_d))
    for d_ylo in range(2):
        for d_blk in range(4):
            if (d_ylo, d_blk) != (0, 0):
                partners.append(device(lax.rem(ylo + d_ylo, 2), x, z, lax.rem(blk + d_blk, 4)))
    for p in partners:
        pl.semaphore_signal(barrier, inc=1, device_id=p, device_id_type=MESH)
    for cp in loads[1:]:
        cp.start()
    loads[0].wait()
    for h in range(2):
        for core_d in range(2):
            for u in range(2):
                for q in range(2):
                    r, c = 16 * core_d + 8 * u, 256 * h + 128 * q
                    l_buf[core_d, u, 2 * h + q] = l_ref[r : r + 8, c : c + 128]
    pl.semaphore_wait(barrier, len(partners))

    upper = ylo == 0
    spread = [(ylo_d, blk_d) for blk_d in range(4) for ylo_d in range(2)]
    x_to = jnp.where(upper, x, mirror)
    slot_to = jnp.where(upper, 0, 4 - x) + 2 * blk
    tiles_out = jnp.clip(jnp.where(upper, x, 4 + x) + 1 - 2 * blk, 0, 2)

    def spread_copy(n, ylo_d, blk_d):
        return (
            l_buf.at[blk_d % 2, :, pl.ds(0, 2 * n)], z_own.at[0, :, pl.ds(2 * slot_to, 2 * n)],
            l_send.at[ylo_d, blk_d], l_recv.at[jnp.where(upper, blk, 2 + blk)], device(ylo_d, x_to, z, blk_d),
        )

    def spread_mine(ylo_d, blk_d):
        return upper & (ylo_d == ylo) & (blk_d == blk)

    for n in (1, 2):

        @pl.when(tiles_out == n)
        def _():
            for key in spread:
                mine = spread_mine(*key)

                @pl.when(jnp.logical_not(mine))
                def _():
                    copy(*spread_copy(n, *key)).start()

                @pl.when(mine)
                def _():
                    src, dst, _, sem, _ = spread_copy(n, *key)
                    pltpu.make_async_copy(src, dst, sem).start()

    loads[1].wait()
    row = lax.broadcasted_iota(jnp.int32, (8, 128), 0)
    choices = jnp.zeros((8, 128), jnp.int32)
    for i in range(4):
        choices = jnp.where(row == i, sel_own[0, i], choices)
    sel_ref[...] = choices
    sel_copies = []
    for d in range(1, 4):
        cp = copy(
            sel_ref, sel_buf.at[4 - d], sel_send.at[d], sel_recv.at[4 - d],
            device(ylo, lax.rem(x + d, 4), z, blk),
        )
        cp.start()
        sel_copies.append(cp)
    own_sel = pltpu.make_async_copy(sel_ref, sel_buf.at[0], sel_recv.at[0])
    own_sel.start()

    def f_rows(r):
        return pl.ds(256 * r, 256)

    def f_copy(kind, r):
        if kind == 0:
            return copy(f_ref.at[f_rows(r)], f_buf.at[blk, f_rows(r)], fc_send.at[0, r], fc_recv.at[0, r], mate)
        if kind == 1:
            return copy(f_ref.at[f_rows(r)], f_buf.at[blk, f_rows(r)], fc_send.at[1, r], fc_recv.at[1, r], across)
        return copy(
            f_buf.at[across_blk, f_rows(r)], f_buf.at[across_blk, f_rows(r)], fc_send.at[2, r], fc_recv.at[2, r], mate
        )

    def c_copy(kind, r):
        if kind == 0:
            return copy(c_ref.at[f_rows(r)], c_buf.at[blk, f_rows(r)], cc_send.at[0, r], cc_recv.at[0, r], mate)
        if kind == 1:
            return copy(c_ref.at[f_rows(r)], c_buf.at[blk, f_rows(r)], cc_send.at[1, r], cc_recv.at[1, r], across)
        return copy(
            c_buf.at[across_blk, f_rows(r)], c_buf.at[across_blk, f_rows(r)], cc_send.at[2, r], cc_recv.at[2, r], mate
        )

    f_own = [pltpu.make_async_copy(f_ref.at[f_rows(r)], f_buf.at[blk, f_rows(r)], fc_recv.at[3, r]) for r in range(4)]
    c_own = [pltpu.make_async_copy(c_ref.at[f_rows(r)], c_buf.at[blk, f_rows(r)], cc_recv.at[3, r]) for r in range(2)]

    for kind in (1, 0):
        for r in range(4):

            @pl.when(r >= blk)
            def _():
                f_copy(kind, r).start()

    for r in range(4):

        @pl.when(r >= blk)
        def _():
            f_own[r].start()

    for r in range(2):
        c_copy(0, r).start()
        c_own[r].start()

    for cp in loads[2:]:
        cp.wait()

    @pl.loop(0, 16)
    def _(i):
        rows = lax.broadcasted_iota(jnp.int32, (64, 512), 0) + i * 64
        acc = jnp.zeros((64, 512), jnp.float32)
        for k in range(6):
            acc = acc + jnp.where(rows == jci_ref[k : k + 1, :], jcv_ref[k : k + 1, :], 0.0)
        at = pl.ds(pl.multiple_of(i * 64, 64), 64)
        j_high[at, :], j_low[at, :] = split(acc)

    for source in range(6):
        half, b = source // 2 > 0, source if source < 2 else source - 2
        tiles_in = jnp.clip((7 - x if half else x) + 1 - 2 * b, 0, 2)
        first = (x + 1 if half else 0) + 2 * b
        for n in (1, 2):

            @pl.when(tiles_in == n)
            def _():
                area = z_own.at[0, :, pl.ds(2 * first, 2 * n)]
                pltpu.make_async_copy(area, area, l_recv.at[source]).wait()

    def sub(ref, s, u):
        return ref.at[s, u // (PIECES // 2), pl.ds(u % (PIECES // 2) * (2 * TILES // PIECES), 2 * TILES // PIECES)]

    z_copies = []

    def ring(s, u, way):
        to = s + 1 if way == 0 else (s + 7) % 8
        cp = copy(sub(z_own, s, u), sub(z_own, to, u), z_send.at[way, s, u], z_recv.at[to, u], right if way == 0 else left)
        cp.start()
        z_copies.append(cp)

    def share(s):
        cp = copy(z_own.at[s], z_oth.at[s], d_send.at[s], d_recv.at[s], mate)
        cp.start()
        return cp

    shares = []

    def arrived(s, u):
        pltpu.make_async_copy(sub(z_own, s, u), sub(z_own, s, u), z_recv.at[s, u]).wait()

    for u in range(PIECES):
        ring(0, u, 0)
        ring(0, PIECES - 1 - u, 1)
    shares.append(share(0))
    for s in range(1, 4):
        if s == CROSS_AT:
            for r in range(2):
                c_copy(1, r).start()
        for u in range(PIECES):
            arrived(s, u)
            if s < 3 or u < PIECES // 2:
                ring(s, u, 0)
            w = PIECES - 1 - u
            arrived(8 - s, w)
            if s < 3 or w >= PIECES // 2:
                ring(8 - s, w, 1)
        shares.append(share(s))
        shares.append(share(8 - s))
    for v in range(PIECES // 2):
        for u in (v, PIECES - 1 - v):
            arrived(4, u)
    shares.append(share(4))
    for cp in sel_copies:
        cp.wait()
    own_sel.wait()
    pltpu.sync_copy(sel_buf, sel_sm)
    for cp in shares:
        cp.wait()

    row_is = lax.broadcasted_iota(jnp.int32, (128, 128), 0)
    col_is = lax.broadcasted_iota(jnp.int32, (128, 128), 1)

    def gram(d):
        for i in range(4):
            j = sel_sm[d, lax.rem(i + core, 4), 0]
            choice = sel_buf[d, pl.ds(lax.rem(i + core, 4), 1), :]
            last0 = 2 * x + 1
            last1 = 15 - 2 * x
            below = 2 * (x + 1) + jnp.minimum(j, last1)
            at = slice(128 * i, 128 * i + 128)
            for n, ref in enumerate((z_own, z_oth)):
                part = ref[:, :, j].reshape(128, 128)
                s_high[256 * n : 256 * n + 128, at], s_low[256 * n : 256 * n + 128, at] = split(
                    jnp.where(choice <= last0, part, 0.0)
                )
                part = ref[:, :, below].reshape(128, 128)
                s_high[256 * n + 128 : 256 * n + 256, at], s_low[256 * n + 128 : 256 * n + 256, at] = split(
                    jnp.where(choice <= last1, part, 0.0)
                )

        def cols(a, b):
            return s_high[:, a:b], s_low[:, a:b]

        first = dot(cols(0, 128), cols(0, 384), axis=0)
        second = dot(cols(256, 384), cols(256, 512), axis=0)
        a_send[d, 0:128, 0:128] = jnp.where(
            row_is > col_is, 2.0 * first[:, 0:128], jnp.where(row_is == col_is, first[:, 0:128], 2.0 * second[:, 0:128])
        )
        a_send[d, 128:136, 0:128] = jnp.broadcast_to(
            jnp.sum(jnp.where(row_is == col_is, second[:, 0:128], 0.0), axis=0, keepdims=True), (8, 128)
        )
        a_send[d, 0:128, 128:384] = 2.0 * first[:, 128:384]
        a_send[d, 0:128, 384:512] = 2.0 * second[:, 128:256]

    x_next = device(ylo, lax.rem(x + 1, 4), z, blk)
    x_last = device(ylo, lax.rem(x + 3, 4), z, blk)
    top, bottom = pl.ds(0, 64), pl.ds(64, 72)
    x_copies = [
        copy(a_send.at[2, top], a_pass.at[pl.ds(0, 64)], x_send.at[0], x_recv.at[0], x_next),
        copy(a_send.at[2, bottom], a_pass.at[pl.ds(64, 72)], x_send.at[1], x_recv.at[1], x_last),
        copy(a_send.at[1, bottom], a_recv.at[0, bottom], x_send.at[2], x_recv.at[2], x_next),
        copy(a_send.at[3, top], a_recv.at[1, top], x_send.at[3], x_recv.at[3], x_last),
        copy(a_send.at[1, top], a_recv.at[0, top], x_send.at[4], x_recv.at[4], x_next),
        copy(a_send.at[3, bottom], a_recv.at[1, bottom], x_send.at[5], x_recv.at[5], x_last),
    ]
    gram(2)
    x_copies[0].start()
    x_copies[1].start()
    gram(1)
    x_copies[2].start()
    for r in range(4):

        @pl.when(r >= across_blk)
        def _():
            f_copy(1, r).wait_recv()
            f_copy(2, r).start()

    gram(3)
    x_copies[3].start()
    gram(0)
    x_copies[0].wait_recv()
    a_send[1, 0:64, :] = a_send[1, 0:64, :] + a_pass[0:64, :]
    x_copies[4].start()
    x_copies[1].wait_recv()
    a_send[3, 64:136, :] = a_send[3, 64:136, :] + a_pass[64:136, :]
    x_copies[5].start()

    for r in range(4):

        @pl.when(r >= blk)
        def _():
            f_own[r].wait()

        @pl.when(r >= mate_blk)
        def _():
            f_copy(0, r).wait_recv()

        @pl.when(r >= far_blk)
        def _():
            f_copy(2, r).wait_recv()

    square = jnp.zeros((1, 512), jnp.float32)
    for r in range(4):
        rows = slice(256 * r, 256 * r + 256)
        acc = jnp.zeros((256, 512), jnp.float32)
        for s in range(r + 1):
            at = slice(256 * s, 256 * s + 256)
            acc = acc + dot(split(f_buf[s, rows, :]), (j_high[at, :], j_low[at, :]))
        v_high[rows, :], v_low[rows, :] = split(acc)
        square = square + jnp.sum(acc * acc, axis=0, keepdims=True)
        if r == 2:
            for r in range(2):
                c_copy(1, r).wait_recv()
                c_copy(2, r).start()

    for q in range(4):
        if q % 2 == 0:
            c_own[q // 2].wait()
            c_copy(0, q // 2).wait_recv()
            c_copy(2, q // 2).wait_recv()
        rows = lax.broadcasted_iota(jnp.int32, (128, 512), 0) + q * 128
        root = jnp.zeros((128, 512), jnp.float32)
        for k in range(2):
            root = root + jnp.where(rows == jri_ref[k : k + 1, :], jrv_ref[k : k + 1, :], 0.0)
        acc = -root
        for s in range(4):
            at = slice(256 * s, 256 * s + 256)
            acc = acc + dot(split(c_buf[s, 128 * q : 128 * q + 128, :]), (v_high[at, :], v_low[at, :]))
        at = slice(128 * q, 128 * q + 128)
        g_buf[at, :] = acc
        g_high[at, :], g_low[at, :] = split(acc)
        if q == 0:
            g_buf[512:640, :] = acc
            g_high[512:640, :], g_low[512:640, :] = split(acc)

    for cp in x_copies[2:]:
        cp.wait_recv()
    a_sum[0] = a_send[0] + a_recv[0] + a_recv[1]
    a_share = copy(a_sum.at[0], a_sum.at[1], as_send, as_recv, mate)
    a_share.start()

    def quad(n, c):
        both = a_sum[n, 0:128, 0:128]
        lower = jnp.where(row_is >= col_is, both, 0.0)
        diagonal = jnp.where(row_is == col_is, a_sum[n, 128:129, 0:128], 0.0)
        upper_ = jnp.where(row_is < col_is, both, diagonal)
        total = jnp.zeros((1, 512), jnp.float32)
        for corner, a, b, off in ((lower, 128, 384, 0), (upper_, 384, 512, 256)):
            start = pl.multiple_of(c * 128 + off, 128)
            near_ = pl.ds(start, 128)
            after = pl.ds(pl.multiple_of(start + 128, 128), b - a)
            w = dot(split(corner), (g_high[near_, :], g_low[near_, :]))
            w = w + dot(split(a_sum[n, 0:128, a:b]), (g_high[after, :], g_low[after, :]))
            total = total + jnp.sum(w * g_buf[near_, :], axis=0, keepdims=True)
        return total

    omega = noise_ref[...] + square + quad(0, core)
    a_share.wait()
    omega = omega + quad(1, 1 - core)
    live = lax.broadcasted_iota(jnp.int32, (1, 512), 1) < count_ref[0]
    out_ref[...] = jnp.where(live, resid_ref[...] / jnp.sqrt(omega), 0.0)

    for n in (1, 2):

        @pl.when(tiles_out == n)
        def _():
            for key in spread:

                @pl.when(jnp.logical_not(spread_mine(*key)))
                def _():
                    copy(*spread_copy(n, *key)).wait_send()

    for cp in z_copies:
        cp.wait_send()
    for cp in x_copies:
        cp.wait_send()
    for r in range(4):

        @pl.when(r >= blk)
        def _():
            f_copy(0, r).wait_send()
            f_copy(1, r).wait_send()

        @pl.when(r >= across_blk)
        def _():
            f_copy(2, r).wait_send()

    for r in range(2):
        for kind in range(3):
            c_copy(kind, r).wait_send()


def per_device(root, front, coupling, blocks, jci, jcv, jri, jrv, resid, noise, count):
    vmem = pl.BlockSpec(memory_space=pltpu.VMEM)
    dma = pltpu.SemaphoreType.DMA
    f32, bf16 = jnp.float32, jnp.bfloat16
    out = pl.pallas_call(
        kernel,
        out_shape=jax.ShapeDtypeStruct((1, 512), f32),
        in_specs=[pl.BlockSpec(memory_space=pltpu.HBM)] * 11,
        out_specs=vmem,
        scratch_shapes=[
            pltpu.VMEM((32, 512), f32),
            pltpu.VMEM((8, 128), jnp.int32),
            pltpu.VMEM((6, 512), jnp.int32),
            pltpu.VMEM((6, 512), f32),
            pltpu.VMEM((2, 512), jnp.int32),
            pltpu.VMEM((2, 512), f32),
            pltpu.VMEM((1, 512), f32),
            pltpu.VMEM((1, 512), f32),
            pltpu.SMEM((1, 4), jnp.int32),
            pltpu.SMEM((1,), jnp.int32),
            dma((9,)),
            pltpu.VMEM((2, 2, 4, 8, 128), f32),
            pltpu.VMEM((8, 2, TILES, 8, 128), f32),
            pltpu.VMEM((8, 2, TILES, 8, 128), f32),
            pltpu.VMEM((4, 1024, 256), f32),
            pltpu.VMEM((4, 512, 256), f32),
            pltpu.VMEM((1024, 512), bf16),
            pltpu.VMEM((1024, 512), bf16),
            pltpu.VMEM((1024, 512), bf16),
            pltpu.VMEM((1024, 512), bf16),
            pltpu.VMEM((640, 512), f32),
            pltpu.VMEM((640, 512), bf16),
            pltpu.VMEM((640, 512), bf16),
            pltpu.VMEM((512, 512), bf16),
            pltpu.VMEM((512, 512), bf16),
            pltpu.VMEM((4, 136, 512), f32),
            pltpu.VMEM((136, 512), f32),
            pltpu.VMEM((2, 136, 512), f32),
            pltpu.VMEM((2, 136, 512), f32),
            pltpu.VMEM((4, 8, 128), jnp.int32),
            pltpu.SMEM((4, 8, 128), jnp.int32),
            dma((2, 4)), dma((6,)), dma((2, 8, PIECES)), dma((8, PIECES)), dma((8,)), dma((8,)),
            dma((4,)), dma((4,)),
            dma((3, 4)), dma((4, 4)), dma((3, 2)), dma((4, 2)),
            dma((6,)), dma((6,)), dma, dma,
        ],
        compiler_params=pltpu.CompilerParams(
            collective_id=0, has_side_effects=True, vmem_limit_bytes=63 << 20
        ),
        name="selected_inverse",
    )(
        root, front, coupling, blocks, jci, jcv, jri, jrv,
        resid.reshape(1, -1), noise.reshape(1, -1), count,
    )
    return out.reshape(-1)


def solution(mesh):
    placed = (
        P("leaf", "blk"),
        P("leaf", "blk"),
        P("leaf", "blk"),
        P("leaf", None),
        P(None, ("leaf", "blk")),
        P(None, ("leaf", "blk")),
        P(None, ("leaf", "blk")),
        P(None, ("leaf", "blk")),
        P(("leaf", "blk")),
        P(("leaf", "blk")),
        P(("leaf", "blk")),
    )
    return jax.shard_map(
        per_device, mesh=mesh, in_specs=placed, out_specs=P(("leaf", "blk")), check_vma=False
    )
```
